256 devices in a mesh: ctx: 32 (over x, z), head: 8 (over y, core).
Axes of the slice: x: 4, y: 4, z: 8, core: 2. Of those that a mesh axis runs over, the one named last changes fastest.
Arguments:
- query: bfloat16 [65536, 8192], P(('ctx', 'head')), as said below
- key: bfloat16 [65536, 1024], P(('ctx', 'head')), as said below
- value: bfloat16 [65536, 1024], P(('ctx', 'head')), may hold values from -6 to 6
- doc_ids: int32 [512], replicated, may hold values from 0 to 84, never falling along the last dimension, each value on 1 to 8 neighbouring positions
- plan: int32 [512], replicated, may hold values from 0 to 511, as said below
Outputs:
- attended: bfloat16 [65536, 8192], P('ctx', 'head')
The draws below stay inside these ranges and needn't reach their ends.
Inputs may be any that keep to these rules, and one draw needn't show every extreme that they name: `doc_ids`: block ids never fall; each document holds 1 to 8 blocks, one exactly 8. `plan`: A permutation of the 512 blocks. Output positions k * 16 to (k + 1) * 16 - 1 belong to context shard k. Every shard receives 16 blocks; of the blocks j * 16 to (j + 1) * 16 - 1 at most 1 go to one shard, and exactly 1 to some shard. `query`: real values; no structure promised. `key`: real values; no structure promised.
All inputs are finite; a program needn't handle non-finite values.
Results may differ from the reference program's by a relative error of at most 0.0038.
Values may be sent and summed in bfloat16 or wider, within the bound.
No kernel may reach another device: no remote copies, remote signals or barrier semaphores. Data moves between devices by JAX's collectives and lax.ppermute only.
A program may use at most 128 MiB of HBM per device.

```python
import math
import jax
import jax.numpy as jnp
import numpy as np
from jax import lax

HQ = 64
HK = 8
HD = 128
BLK = 128
BLK_DEV = 16
MAXDOC = 8
NBLK = 512
TOKENS = 65536
NDOC = 85


def key_field(key):
    base = jax.random.fold_in(key, 11)
    first = jax.random.fold_in(base, 0)
    field = jax.random.normal(first, (TOKENS, HK * HD), jnp.float32)
    marks = jnp.zeros((TOKENS,), bool)
    return (field, marks)


def draw_key(key, part):
    field, marks = key_field(key)
    return field.astype(jnp.bfloat16)


def draw_query(key, part):
    field, marks = key_field(key)
    noise_key = jax.random.fold_in(key, 12)
    noise = jax.random.normal(noise_key, (TOKENS, HQ * HD), jnp.float32)
    return jnp.where(marks[:, None], noise, noise).astype(jnp.bfloat16)


def draw_plan(key, part):
    base = jax.random.fold_in(key, 21)
    first, second, third, fourth = jax.random.split(base, 4)
    shards = NBLK // BLK_DEV
    ranks = jax.random.permutation(first, shards)
    offsets = ranks[jnp.arange(BLK_DEV) % shards]
    sigma = jax.random.permutation(second, shards)
    raw = jax.random.randint(third, (shards, BLK_DEV), 0, 1048576) * BLK_DEV + jnp.arange(BLK_DEV)[None, :]
    local_order = jnp.argsort(raw, axis=1, stable=True)
    sources = jnp.arange(shards)[:, None]
    target = sigma[(sources + offsets[local_order]) % shards]
    mixing = jax.random.permutation(fourth, NBLK)
    sort_key = target.reshape(NBLK) * NBLK + mixing
    return jnp.argsort(sort_key, stable=True).astype(jnp.int32)


def steps_of(stream_key, dims, cuts, low, high):
    def one(axis_at, blocks):
        draws = jax.random.uniform(jax.random.fold_in(jax.random.fold_in(stream_key, 6), axis_at), (blocks,), jnp.float32, low / len(cuts), high / len(cuts))
        return jnp.repeat(jnp.exp(draws), dims[axis_at] // blocks).reshape((-1,) + (1,) * (len(dims) - axis_at - 1))

    factor_of = one(*cuts[0])
    for cut in cuts[1:]:
        factor_of = factor_of * one(*cut)
    return factor_of


def length_profile(number_of, total, reach, lean):
    weights = [(1 << 20) // math.isqrt(rank ** lean) + 1 for rank in range(2, number_of + 1)]
    surplus, counts = total - reach - (number_of - 1), [1] * (number_of - 1)
    while surplus > 0:
        free = [i for i in range(number_of - 1) if counts[i] < reach]
        whole, budget = sum([weights[i] for i in free]), surplus
        for i in free:
            extra = min(reach - counts[i], max(1, budget * weights[i] // whole), surplus)
            counts[i] = counts[i] + extra
            surplus = surplus - extra
    return np.array([reach] + counts)


def uneven(rng, number_of, total, bound, lean):
    if number_of == 2:
        one = jax.random.randint(rng, (), max(1, total - bound), min(bound, total - 1) + 1)
        return jnp.stack([one, total - one])
    tallies = jnp.asarray(length_profile(number_of, total, bound, lean), jnp.int32)
    pairs = (number_of - 1) // 2
    giver, receiver = tallies[1:1 + 2 * pairs:2], tallies[2:2 + 2 * pairs:2]
    slack = jnp.minimum(giver - 1, bound - receiver)
    moved = jax.random.randint(jax.random.fold_in(rng, 1), (pairs,), 0, 1 << 20) % (slack + 1)
    tallies = tallies.at[1:1 + 2 * pairs:2].set(giver - moved).at[2:2 + 2 * pairs:2].set(receiver + moved)
    return tallies[jax.random.permutation(jax.random.fold_in(rng, 2), number_of)]


def bell_draw(key, extent, scale, most, cuts=(), held_as=jnp.bfloat16):
    drawn = jax.random.normal(key, extent, jnp.float32) * scale
    if len(cuts) > 0:
        drawn = steps_of(key, extent, cuts, -0.22, 0.18) * drawn
    return jnp.clip(drawn, min=-most, max=most).astype(held_as)


def setup_inputs(seed: int = 0) -> dict:
    streams_of = jax.random.split(jax.random.key(seed), 6)
    return {
        "query": draw_query(jax.random.fold_in(streams_of[5], 71), 0),
        "key": draw_key(jax.random.fold_in(streams_of[5], 71), 0),
        "value": bell_draw(streams_of[2], (TOKENS, HK * HD), 1.0, 6.0, ((0, 256),)),
        "doc_ids": jnp.searchsorted(jnp.cumsum(uneven(streams_of[3], NDOC, NBLK, MAXDOC, 2)), jnp.arange(NBLK), side="right").astype(jnp.int32),
        "plan": draw_plan(jax.random.fold_in(streams_of[5], 71), 0),
    }


def reference(query, key, value, doc_ids, plan):
    width = HQ * HD
    group = HQ // HK
    window = MAXDOC * BLK
    pad = (MAXDOC - 1) * BLK
    scale = 1.0 / math.sqrt(HD)
    key_pad = jnp.concatenate([jnp.zeros((pad, HK * HD), key.dtype), key], 0)
    value_pad = jnp.concatenate([jnp.zeros((pad, HK * HD), value.dtype), value], 0)
    row_docs = jnp.repeat(doc_ids, BLK)
    doc_pad = jnp.concatenate([jnp.full((pad,), -1, jnp.int32), row_docs.astype(jnp.int32)], 0)

    def one_block(block):
        start = (block * BLK).astype(jnp.int32)
        queries = lax.dynamic_slice_in_dim(query, start, BLK, 0).astype(jnp.float32).reshape(BLK, HK, group, HD)
        keys = lax.dynamic_slice_in_dim(key_pad, start, window, 0).astype(jnp.float32).reshape(window, HK, HD)
        values = lax.dynamic_slice_in_dim(value_pad, start, window, 0).astype(jnp.float32).reshape(window, HK, HD)
        docs = lax.dynamic_slice_in_dim(doc_pad, start, window, 0)
        scores = jnp.einsum('qkgd,skd->kgqs', queries, keys) * scale
        query_pos = start + jnp.arange(BLK, dtype=jnp.int32)
        key_pos = start - pad + jnp.arange(window, dtype=jnp.int32)
        allowed = (docs[None, :] == doc_ids[block]) & (key_pos[None, :] <= query_pos[:, None])
        scores = jnp.where(allowed, scores, -jnp.inf)
        top = lax.optimization_barrier(jnp.max(scores, axis=3, keepdims=True))
        expo = jnp.exp(scores - top)
        total = lax.optimization_barrier(jnp.sum(expo, axis=3))
        weights = lax.optimization_barrier(expo.astype(jnp.bfloat16)).astype(jnp.float32)
        summed = jnp.einsum('kgqs,skd->kgqd', weights, values)
        mixed = summed / total[..., None]
        return mixed.transpose(2, 0, 1, 3).reshape(BLK, width).astype(jnp.bfloat16)
    heads_out = lax.map(one_block, jnp.arange(NBLK, dtype=jnp.int32))
    return heads_out[plan].reshape(TOKENS, width)
```

```python
import functools
import math

import jax
import jax.numpy as jnp
from jax import lax
from jax.experimental import pallas as pl
from jax.experimental.pallas import tpu as pltpu
from jax.sharding import PartitionSpec as P

HD = 128
BLK = 128
MAXDOC = 8
HALO = MAXDOC - 1
CHUNKS = (2, 2, 2, 2)
EXP2_SCALE = math.log2(math.e) / math.sqrt(HD)


def attend_kernel(doc_ref, slot_ref, shard_ref, q_ref, own_ref, halo_ref, out_ref, win_ref, *, heads, count):
    index = pl.program_id(0)

    @pl.when(index == 0)
    def _():
        win_ref[: HALO * BLK, :] = halo_ref[...]
        win_ref[HALO * BLK :, :] = own_ref[...]

    block = shard_ref[0] * count + index
    doc = doc_ref[block]
    tiles = jnp.int32(1)
    for back in range(1, MAXDOC):
        at = jnp.maximum(block - back, 0)
        tiles += jnp.where((block >= back) & (doc_ref[at] == doc), 1, 0)

    row = lax.broadcasted_iota(jnp.int32, (BLK, BLK), 0)
    column = lax.broadcasted_iota(jnp.int32, (BLK, BLK), 1)
    causal = column <= row

    def with_tiles(n):
        start = pl.multiple_of((index + MAXDOC - n) * BLK, BLK)
        keys = win_ref[pl.ds(start, n * BLK), :HD]
        values = win_ref[pl.ds(start, n * BLK), HD:]
        for head in range(heads):
            columns = slice(head * HD, (head + 1) * HD)
            scores = lax.dot_general(
                q_ref[:, columns], keys, (((1,), (1,)), ((), ())), preferred_element_type=jnp.float32
            )
            last = jnp.where(causal, scores[:, (n - 1) * BLK :], -jnp.inf)
            if n > 1:
                scores = jnp.concatenate([scores[:, : (n - 1) * BLK], last], axis=1)
            else:
                scores = last
            top = jnp.max(scores, axis=1, keepdims=True)
            expo = jnp.exp2((scores - top) * EXP2_SCALE)
            total = jnp.sum(expo, axis=1, keepdims=True)
            mixed = jnp.dot(expo.astype(jnp.bfloat16), values, preferred_element_type=jnp.float32)
            out_ref[0, :, columns] = (mixed / total).astype(jnp.bfloat16)

    for n in range(1, MAXDOC + 1):
        pl.when(tiles == n)(functools.partial(with_tiles, n))


def attend(queries, kv_own, kv_halo, doc_ids, slot, shard, slots):
    rows, width = queries.shape
    count = rows // BLK
    heads = width // HD
    return pl.pallas_call(
        functools.partial(attend_kernel, heads=heads, count=count),
        grid_spec=pltpu.PrefetchScalarGridSpec(
            num_scalar_prefetch=3,
            grid=(count,),
            in_specs=[
                pl.BlockSpec((BLK, width), lambda i, doc, slot, shard: (i, 0)),
                pl.BlockSpec(kv_own.shape, lambda i, doc, slot, shard: (0, 0)),
                pl.BlockSpec(kv_halo.shape, lambda i, doc, slot, shard: (0, 0)),
            ],
            out_specs=pl.BlockSpec((1, BLK, width), lambda i, doc, slot, shard: (slot[i], 0, 0)),
            scratch_shapes=[pltpu.VMEM((kv_own.shape[0] + kv_halo.shape[0], 2 * HD), jnp.bfloat16)],
        ),
        out_shape=jax.ShapeDtypeStruct((slots, BLK, width), jnp.bfloat16),
        compiler_params=pltpu.CompilerParams(vmem_limit_bytes=32 * 1024 * 1024),
        cost_estimate=pl.CostEstimate(
            flops=4 * rows * heads * HD * BLK * 4,
            bytes_accessed=4 * rows * width + 4 * kv_own.size,
            transcendentals=rows * heads * BLK * 4,
        ),
        name="attend",
    )(doc_ids, slot, shard, queries, kv_own, kv_halo)


def place_kernel(source_ref, *refs, count, first, width):
    received_ref, out_ref, sems = refs[0], refs[-2], refs[-1]

    def copy(i):
        return pltpu.make_async_copy(
            received_ref.at[source_ref[i]],
            out_ref.at[pl.ds(i * BLK, BLK), pl.ds(first, width)],
            sems.at[i],
        )

    for i in range(count):
        copy(i).start()
    for i in range(count):
        copy(i).wait()


def place(received, source, result, first, count, full_width):
    slots, _, width = received.shape
    given = [received] if result is None else [received, result]
    return pl.pallas_call(
        functools.partial(place_kernel, count=count, first=first, width=width),
        in_specs=[pl.BlockSpec(memory_space=pltpu.SMEM)] + [pl.BlockSpec(memory_space=pl.ANY)] * len(given),
        out_specs=pl.BlockSpec(memory_space=pl.ANY),
        out_shape=jax.ShapeDtypeStruct((count * BLK, full_width), jnp.bfloat16),
        scratch_shapes=[pltpu.SemaphoreType.DMA((count,))],
        input_output_aliases={} if result is None else {2: 0},
        cost_estimate=pl.CostEstimate(flops=0, bytes_accessed=4 * count * BLK * width, transcendentals=0),
        name="place",
    )(source, *given)


def shards(query, key, value, doc_ids, plan):
    head_count = lax.axis_size("head")
    shard_count = lax.axis_size("ctx")
    local_rows = query.shape[0]
    rows = head_count * local_rows
    count = rows // BLK
    q_width = query.shape[1] // head_count
    shard = lax.axis_index("ctx").astype(jnp.int32)

    def to_heads(parts):
        moved = lax.all_to_all(parts.transpose(1, 0, 2), "head", split_axis=0, concat_axis=0, tiled=True)
        return moved.reshape(rows, parts.shape[2])

    kv_parts = jnp.concatenate(
        [key.reshape(local_rows, head_count, HD), value.reshape(local_rows, head_count, HD)], axis=2
    )
    kv_own = to_heads(kv_parts)
    kv_halo = lax.ppermute(
        kv_own[rows - HALO * BLK :], "ctx", [(i, i + 1) for i in range(shard_count - 1)]
    )

    own_ids = shard * count + jnp.arange(count, dtype=jnp.int32)
    position = jnp.arange(plan.shape[0], dtype=jnp.int32)
    target = jnp.sum(
        jnp.where(plan[None, :] == own_ids[:, None], position[None, :] // count, 0), axis=1, dtype=jnp.int32
    )
    source = lax.dynamic_slice_in_dim(plan, shard * count, count) // count

    q_parts = query.reshape(local_rows, head_count, q_width)
    result = None
    first = 0
    for heads in CHUNKS:
        width = heads * HD
        queries = to_heads(q_parts[:, :, first : first + width])
        sent = attend(queries, kv_own, kv_halo, doc_ids, target, shard.reshape(1), shard_count)
        received = lax.all_to_all(sent, "ctx", split_axis=0, concat_axis=0, tiled=True)
        result = place(received, source, result, first, count, q_width)
        first += width
    return result


def solution(mesh):
    return jax.shard_map(
        shards,
        mesh=mesh,
        in_specs=(
            P(("ctx", "head"), None),
            P(("ctx", "head"), None),
            P(("ctx", "head"), None),
            P(),
            P(),
        ),
        out_specs=P("ctx", "head"),
        check_vma=False,
    )
```

```python
import functools
import math

import jax
import jax.numpy as jnp
from jax import lax
from jax.experimental import pallas as pl
from jax.experimental.pallas import tpu as pltpu
from jax.sharding import PartitionSpec as P

HD = 128
BLK = 128
MAXDOC = 8
HALO = MAXDOC - 1
CHUNKS = (1, 2, 5)
EXP2_SCALE = math.log2(math.e) / math.sqrt(HD)


def attend_kernel(
    doc_ref, slot_ref, origin_ref, shard_ref, q_ref, own_ref, halo_ref, out_ref, win_ref, *, heads, count
):
    index = pl.program_id(0)

    @pl.when(index == 0)
    def _():
        win_ref[: HALO * BLK, :] = halo_ref[...]
        win_ref[HALO * BLK :, :] = own_ref[...]

    block = shard_ref[0] * count + index
    doc = doc_ref[block]
    tiles = jnp.int32(1)
    for back in range(1, MAXDOC):
        at = jnp.maximum(block - back, 0)
        tiles += jnp.where((block >= back) & (doc_ref[at] == doc), 1, 0)

    row = lax.broadcasted_iota(jnp.int32, (BLK, BLK), 0)
    column = lax.broadcasted_iota(jnp.int32, (BLK, BLK), 1)
    causal = column <= row

    def with_tiles(n):
        start = pl.multiple_of((index + MAXDOC - n) * BLK, BLK)
        keys = win_ref[pl.ds(start, n * BLK), :HD]
        values = win_ref[pl.ds(start, n * BLK), HD:]
        for head in range(heads):
            columns = slice(head * HD, (head + 1) * HD)
            scores = lax.dot_general(
                q_ref[:, columns], keys, (((1,), (1,)), ((), ())), preferred_element_type=jnp.float32
            )
            last = jnp.where(causal, scores[:, (n - 1) * BLK :], -jnp.inf)
            if n > 1:
                scores = jnp.concatenate([scores[:, : (n - 1) * BLK], last], axis=1)
            else:
                scores = last
            top = jnp.max(scores, axis=1, keepdims=True)
            expo = jnp.exp2((scores - top) * EXP2_SCALE)
            total = jnp.sum(expo, axis=1, keepdims=True)
            mixed = jnp.dot(expo.astype(jnp.bfloat16), values, preferred_element_type=jnp.float32)
            out_ref[0, :, columns] = (mixed / total).astype(jnp.bfloat16)

    for n in range(1, MAXDOC + 1):
        pl.when(tiles == n)(functools.partial(with_tiles, n))


def attend(queries, kv_own, kv_halo, doc_ids, slot, origin, shard, slots):
    rows, width = queries.shape
    count = rows // BLK
    heads = width // HD
    return pl.pallas_call(
        functools.partial(attend_kernel, heads=heads, count=count),
        grid_spec=pltpu.PrefetchScalarGridSpec(
            num_scalar_prefetch=4,
            grid=(count,),
            in_specs=[
                pl.BlockSpec((BLK, width), lambda i, doc, slot, origin, shard: (origin[i], 0)),
                pl.BlockSpec(kv_own.shape, lambda i, doc, slot, origin, shard: (0, 0)),
                pl.BlockSpec(kv_halo.shape, lambda i, doc, slot, origin, shard: (0, 0)),
            ],
            out_specs=pl.BlockSpec((1, BLK, width), lambda i, doc, slot, origin, shard: (slot[i], 0, 0)),
            scratch_shapes=[pltpu.VMEM((kv_own.shape[0] + kv_halo.shape[0], 2 * HD), jnp.bfloat16)],
        ),
        out_shape=jax.ShapeDtypeStruct((slots, BLK, width), jnp.bfloat16),
        compiler_params=pltpu.CompilerParams(vmem_limit_bytes=32 * 1024 * 1024),
        cost_estimate=pl.CostEstimate(
            flops=4 * rows * heads * HD * BLK * 4,
            bytes_accessed=4 * rows * width + 4 * kv_own.size,
            transcendentals=rows * heads * BLK * 4,
        ),
        name="attend",
    )(doc_ids, slot, origin, shard, queries, kv_own, kv_halo)


def place_kernel(source_ref, *refs, count, first, width):
    received_ref, out_ref, held_ref, in_sems, out_sems = refs[0], refs[-4], refs[-3], refs[-2], refs[-1]

    def fetch(i):
        return pltpu.make_async_copy(received_ref.at[source_ref[i]], held_ref.at[i], in_sems.at[i])

    def store(i):
        return pltpu.make_async_copy(
            held_ref.at[i], out_ref.at[pl.ds(i * BLK, BLK), pl.ds(first, width)], out_sems.at[i]
        )

    for i in range(count):
        fetch(i).start()
    for i in range(count):
        fetch(i).wait()
        store(i).start()
    for i in range(count):
        store(i).wait()


def place(received, source, result, first, count, full_width):
    slots, _, width = received.shape
    given = [received] if result is None else [received, result]
    return pl.pallas_call(
        functools.partial(place_kernel, count=count, first=first, width=width),
        in_specs=[pl.BlockSpec(memory_space=pltpu.SMEM)] + [pl.BlockSpec(memory_space=pl.ANY)] * len(given),
        out_specs=pl.BlockSpec(memory_space=pl.ANY),
        out_shape=jax.ShapeDtypeStruct((count * BLK, full_width), jnp.bfloat16),
        scratch_shapes=[
            pltpu.VMEM((count, BLK, width), jnp.bfloat16),
            pltpu.SemaphoreType.DMA((count,)),
            pltpu.SemaphoreType.DMA((count,)),
        ],
        input_output_aliases={} if result is None else {2: 0},
        compiler_params=pltpu.CompilerParams(vmem_limit_bytes=32 * 1024 * 1024),
        cost_estimate=pl.CostEstimate(flops=0, bytes_accessed=4 * count * BLK * width, transcendentals=0),
        name="place",
    )(source, *given)


def shards(query, key, value, doc_ids, plan):
    head_count = lax.axis_size("head")
    shard_count = lax.axis_size("ctx")
    local_rows = query.shape[0]
    rows = head_count * local_rows
    count = rows // BLK
    per_device = local_rows // BLK
    q_width = query.shape[1] // head_count
    kv_width = key.shape[1] // head_count
    shard = lax.axis_index("ctx").astype(jnp.int32)
    member = lax.axis_index("head").astype(jnp.int32)
    core, chip, chips = member % 2, member // 2, head_count // 2

    def by_head(array, width, first, size):
        return jnp.stack([array[:, h * width + first : h * width + first + size] for h in range(head_count)])

    def exchange(parts):
        moved = lax.all_to_all(parts, "head", split_axis=0, concat_axis=0, tiled=True)
        return moved.reshape(rows, parts.shape[2])

    def core_swap(parts):
        pairs = parts.reshape(chips, 2, local_rows, parts.shape[2])
        kept = lax.dynamic_index_in_dim(pairs, core, 1, False)
        given = lax.dynamic_index_in_dim(pairs, 1 - core, 1, False)
        got = lax.ppermute(given, "head", [(h, h ^ 1) for h in range(head_count)])
        return jnp.stack([kept, got], axis=1)

    def chip_exchange(both):
        arrived = []
        for step in range(chips):
            piece = lax.dynamic_index_in_dim(both, (chip + step) % chips, 0, False)
            if step:
                piece = lax.ppermute(
                    piece, "head", [(h, (h + 2 * step) % head_count) for h in range(head_count)]
                )
            arrived.append(piece)
        return jnp.stack(arrived).reshape(rows, both.shape[3])

    kv_own = exchange(
        jnp.concatenate([by_head(key, kv_width, 0, kv_width), by_head(value, kv_width, 0, kv_width)], axis=2)
    )
    kv_halo = lax.ppermute(
        kv_own[rows - HALO * BLK :], "ctx", [(i, i + 1) for i in range(shard_count - 1)]
    )

    index = jnp.arange(count, dtype=jnp.int32)
    own_ids = shard * count + index
    position = jnp.arange(plan.shape[0], dtype=jnp.int32)
    target = jnp.sum(
        jnp.where(plan[None, :] == own_ids[:, None], position[None, :] // count, 0), axis=1, dtype=jnp.int32
    )
    source = lax.dynamic_slice_in_dim(plan, shard * count, count) // count
    giver = index // per_device
    steps_back = (chip - giver // 2 + chips) % chips
    arrival = (steps_back * 2 + jnp.where(giver % 2 == core, 0, 1)) * per_device + index % per_device

    result = None
    first = 0
    earlier = kv_own
    for turn, heads in enumerate(CHUNKS):
        width = heads * HD
        parts = by_head(query, q_width, first, width)
        if turn == 0:
            queries = exchange(parts)
            origin = index
        else:
            both, earlier = lax.optimization_barrier((core_swap(parts), earlier))
            queries = chip_exchange(both)
            origin = arrival
        sent = attend(queries, kv_own, kv_halo, doc_ids, target, origin, shard.reshape(1), shard_count)
        earlier = queries if turn == 0 else earlier
        received = lax.all_to_all(sent, "ctx", split_axis=0, concat_axis=0, tiled=True)
        result = place(received, source, result, first, count, q_width)
        first += width
    return result


def solution(mesh):
    return jax.shard_map(
        shards,
        mesh=mesh,
        in_specs=(
            P(("ctx", "head"), None),
            P(("ctx", "head"), None),
            P(("ctx", "head"), None),
            P(),
            P(),
        ),
        out_specs=P("ctx", "head"),
        check_vma=False,
    )
```

```python
import functools
import math

import jax
import jax.numpy as jnp
from jax import lax
from jax.experimental import pallas as pl
from jax.experimental.pallas import tpu as pltpu
from jax.sharding import PartitionSpec as P

HD = 128
BLK = 128
MAXDOC = 8
HALO = MAXDOC - 1
CHUNKS = (1, 2, 5)
EXP2_SCALE = math.log2(math.e) / math.sqrt(HD)


def attend_kernel(doc_ref, slot_ref, origin_ref, shard_ref, q_ref, *refs, heads, count, base, ahead):
    own_ref, win_ref, out_ref = refs[0], refs[-1], refs[-2]
    step = pl.program_id(0)
    index = base + step

    @pl.when(step == 0)
    def _():
        if ahead:
            win_ref[: ahead * BLK, :] = refs[1][...]
        win_ref[ahead * BLK :, :] = own_ref[...]

    block = shard_ref[0] * count + index
    doc = doc_ref[block]
    tiles = jnp.int32(1)
    for back in range(1, MAXDOC):
        at = jnp.maximum(block - back, 0)
        tiles += jnp.where((block >= back) & (doc_ref[at] == doc), 1, 0)

    row = lax.broadcasted_iota(jnp.int32, (BLK, BLK), 0)
    column = lax.broadcasted_iota(jnp.int32, (BLK, BLK), 1)
    causal = column <= row

    def with_tiles(n):
        start = pl.multiple_of((index + ahead + 1 - n) * BLK, BLK)
        keys = win_ref[pl.ds(start, n * BLK), :HD]
        values = win_ref[pl.ds(start, n * BLK), HD:]
        for head in range(heads):
            columns = slice(head * HD, (head + 1) * HD)
            scores = lax.dot_general(
                q_ref[:, columns], keys, (((1,), (1,)), ((), ())), preferred_element_type=jnp.float32
            )
            last = jnp.where(causal, scores[:, (n - 1) * BLK :], -jnp.inf)
            if n > 1:
                scores = jnp.concatenate([scores[:, : (n - 1) * BLK], last], axis=1)
            else:
                scores = last
            top = jnp.max(scores, axis=1, keepdims=True)
            expo = jnp.exp2((scores - top) * EXP2_SCALE)
            total = jnp.sum(expo, axis=1, keepdims=True)
            mixed = jnp.dot(expo.astype(jnp.bfloat16), values, preferred_element_type=jnp.float32)
            out_ref[0, :, columns] = (mixed / total).astype(jnp.bfloat16)

    for n in range(1, MAXDOC + 1):
        pl.when(tiles == n)(functools.partial(with_tiles, n))


def attend(queries, q_column, heads, own, halo, tables, count, slots, base=0, steps=None, result=None):
    doc_ids, slot, origin, shard = tables
    steps = count if steps is None else steps
    width = heads * HD
    ahead = 0 if halo is None else HALO
    own_blocks = base + steps
    given = [queries, own] + ([] if halo is None else [halo]) + ([] if result is None else [result])
    in_specs = [
        pl.BlockSpec((BLK, width), lambda i, doc, slot, origin, shard: (origin[base + i], q_column)),
        pl.BlockSpec((own_blocks * BLK, 2 * HD), lambda i, *_: (0, 0)),
    ]
    if halo is not None:
        in_specs.append(pl.BlockSpec(halo.shape, lambda i, *_: (0, 0)))
    if result is not None:
        in_specs.append(pl.BlockSpec(memory_space=pl.ANY))
    return pl.pallas_call(
        functools.partial(attend_kernel, heads=heads, count=count, base=base, ahead=ahead),
        grid_spec=pltpu.PrefetchScalarGridSpec(
            num_scalar_prefetch=4,
            grid=(steps,),
            in_specs=in_specs,
            out_specs=pl.BlockSpec((1, BLK, width), lambda i, doc, slot, origin, shard: (slot[base + i], 0, 0)),
            scratch_shapes=[pltpu.VMEM(((own_blocks + ahead) * BLK, 2 * HD), jnp.bfloat16)],
        ),
        out_shape=jax.ShapeDtypeStruct((slots, BLK, width), jnp.bfloat16),
        input_output_aliases={} if result is None else {4 + len(given) - 1: 0},
        compiler_params=pltpu.CompilerParams(vmem_limit_bytes=32 * 1024 * 1024),
        cost_estimate=pl.CostEstimate(
            flops=4 * steps * BLK * heads * HD * BLK * 4,
            bytes_accessed=4 * steps * BLK * width + 4 * own_blocks * BLK * HD,
            transcendentals=steps * BLK * heads * BLK * 4,
        ),
        name="attend",
    )(doc_ids, slot, origin, shard, *given)


def first_parts_kernel(k_ref, v_ref, q_ref, out_ref):
    width = k_ref.shape[1]
    out_ref[0, :, :width] = k_ref[...]
    out_ref[0, :, width : 2 * width] = v_ref[...]
    out_ref[0, :, 2 * width :] = q_ref[...]


def first_parts(key, value, query, head_count, width):
    rows = query.shape[0]
    kv_width, q_width = key.shape[1] // head_count, query.shape[1] // head_count
    return pl.pallas_call(
        first_parts_kernel,
        grid=(head_count,),
        in_specs=[
            pl.BlockSpec((rows, kv_width), lambda h: (0, h)),
            pl.BlockSpec((rows, kv_width), lambda h: (0, h)),
            pl.BlockSpec((rows, width), lambda h: (0, h * (q_width // width))),
        ],
        out_specs=pl.BlockSpec((1, rows, 2 * kv_width + width), lambda h: (h, 0, 0)),
        out_shape=jax.ShapeDtypeStruct((head_count, rows, 2 * kv_width + width), jnp.bfloat16),
        name="first_parts",
    )(key, value, query)


def later_parts_kernel(place_ref, q_ref, *out_refs, firsts):
    core = place_ref[0]
    pairs = len(firsts)

    def write(refs):
        for ref, first in zip(refs, firsts):
            ref[0] = q_ref[:, first : first + ref.shape[2]]

    same = pl.program_id(0) % 2 == core
    pl.when(same)(lambda: write(out_refs[:pairs]))
    pl.when(jnp.logical_not(same))(lambda: write(out_refs[pairs:]))


def later_parts(query, place, head_count, firsts, widths):
    rows, q_width, chips = query.shape[0], query.shape[1] // head_count, head_count // 2
    specs = [
        pl.BlockSpec((1, rows, width), lambda h, place: ((h // 2 + chips - place[1]) % chips, 0, 0))
        for width in widths
    ]
    shapes = [jax.ShapeDtypeStruct((chips, rows, width), jnp.bfloat16) for width in widths]
    outs = pl.pallas_call(
        functools.partial(later_parts_kernel, firsts=firsts),
        grid_spec=pltpu.PrefetchScalarGridSpec(
            num_scalar_prefetch=1,
            grid=(head_count,),
            in_specs=[pl.BlockSpec((rows, q_width), lambda h, place: (0, h))],
            out_specs=specs + specs,
        ),
        out_shape=shapes + shapes,
        name="later_parts",
    )(place, query)
    return outs[: len(widths)], outs[len(widths) :]


def place_kernel(source_ref, *refs, count, first, width):
    received_ref, out_ref, held_ref, in_sems, out_sems = refs[0], refs[-4], refs[-3], refs[-2], refs[-1]

    def fetch(i):
        return pltpu.make_async_copy(received_ref.at[source_ref[i]], held_ref.at[i], in_sems.at[i])

    def store(i):
        return pltpu.make_async_copy(
            held_ref.at[i], out_ref.at[pl.ds(i * BLK, BLK), pl.ds(first, width)], out_sems.at[i]
        )

    for i in range(count):
        fetch(i).start()
    for i in range(count):
        fetch(i).wait()
        store(i).start()
    for i in range(count):
        store(i).wait()


def place(received, source, result, first, count, full_width):
    slots, _, width = received.shape
    given = [received] if result is None else [received, result]
    return pl.pallas_call(
        functools.partial(place_kernel, count=count, first=first, width=width),
        in_specs=[pl.BlockSpec(memory_space=pltpu.SMEM)] + [pl.BlockSpec(memory_space=pl.ANY)] * len(given),
        out_specs=pl.BlockSpec(memory_space=pl.ANY),
        out_shape=jax.ShapeDtypeStruct((count * BLK, full_width), jnp.bfloat16),
        scratch_shapes=[
            pltpu.VMEM((count, BLK, width), jnp.bfloat16),
            pltpu.SemaphoreType.DMA((count,)),
            pltpu.SemaphoreType.DMA((count,)),
        ],
        input_output_aliases={} if result is None else {2: 0},
        compiler_params=pltpu.CompilerParams(vmem_limit_bytes=32 * 1024 * 1024),
        cost_estimate=pl.CostEstimate(flops=0, bytes_accessed=4 * count * BLK * width, transcendentals=0),
        name="place",
    )(source, *given)


def shards(query, key, value, doc_ids, plan):
    head_count = lax.axis_size("head")
    shard_count = lax.axis_size("ctx")
    local_rows = query.shape[0]
    rows = head_count * local_rows
    count = rows // BLK
    per_device = local_rows // BLK
    q_width = query.shape[1] // head_count
    shard = lax.axis_index("ctx").astype(jnp.int32)
    member = lax.axis_index("head").astype(jnp.int32)
    core, chip, chips = member % 2, member // 2, head_count // 2

    widths = [heads * HD for heads in CHUNKS]
    firsts = [sum(widths[:i]) for i in range(len(widths))]
    kept, given = later_parts(query, jnp.stack([core, chip]), head_count, firsts[1:], widths[1:])
    got = [lax.ppermute(part, "head", [(h, h ^ 1) for h in range(head_count)]) for part in given]
    opening = lax.all_to_all(
        first_parts(key, value, query, head_count, widths[0]), "head", split_axis=0, concat_axis=0, tiled=True
    )

    index = jnp.arange(count, dtype=jnp.int32)
    own_ids = shard * count + index
    position = jnp.arange(plan.shape[0], dtype=jnp.int32)
    target = jnp.sum(
        jnp.where(plan[None, :] == own_ids[:, None], position[None, :] // count, 0), axis=1, dtype=jnp.int32
    )
    source = lax.dynamic_slice_in_dim(plan, shard * count, count) // count
    giver = index // per_device
    steps_back = (chip - giver // 2 + chips) % chips
    arrival = (steps_back * 2 + jnp.where(giver % 2 == core, 0, 1)) * per_device + index % per_device

    opening, kept, got, target, source, arrival = lax.optimization_barrier(
        (opening, kept, got, target, source, arrival)
    )
    opening = opening.reshape(rows, 2 * HD + widths[0])
    halo = lax.ppermute(
        opening[rows - HALO * BLK :, : 2 * HD], "ctx", [(i, i + 1) for i in range(shard_count - 1)]
    )
    straight = (doc_ids, target, index, shard.reshape(1))
    arranged = (doc_ids, target, arrival, shard.reshape(1))

    result = None
    for turn, heads in enumerate(CHUNKS):
        if turn == 0:
            column = 2 * HD // widths[0]
            sent = attend(
                opening, column, heads, opening, None, straight, count, shard_count, HALO, count - HALO
            )
            sent = attend(opening, column, heads, opening, halo, straight, count, shard_count, 0, HALO, sent)
        else:
            arrived = []
            for step in range(chips):
                piece = jnp.stack([kept[turn - 1][step], got[turn - 1][step]])
                if step:
                    piece = lax.ppermute(
                        piece, "head", [(h, (h + 2 * step) % head_count) for h in range(head_count)]
                    )
                arrived.append(piece)
            queries = jnp.stack(arrived).reshape(rows, widths[turn])
            sent = attend(queries, 0, heads, opening, halo, arranged, count, shard_count)
        received = lax.all_to_all(sent, "ctx", split_axis=0, concat_axis=0, tiled=True)
        result = place(received, source, result, firsts[turn], count, q_width)
    return result


def solution(mesh):
    return jax.shard_map(
        shards,
        mesh=mesh,
        in_specs=(
            P(("ctx", "head"), None),
            P(("ctx", "head"), None),
            P(("ctx", "head"), None),
            P(),
            P(),
        ),
        out_specs=P("ctx", "head"),
        check_vma=False,
    )
```

```python
import functools
import math

import jax
import jax.numpy as jnp
from jax import lax
from jax.experimental import pallas as pl
from jax.experimental.pallas import tpu as pltpu
from jax.sharding import PartitionSpec as P

HD = 128
BLK = 128
MAXDOC = 8
VMEM_BYTES = 60 * 1024 * 1024
HALO = MAXDOC - 1
CHUNKS = (2, 3, 3)
EXP2_SCALE = math.log2(math.e) / math.sqrt(HD)


def attend_kernel(doc_ref, slot_ref, order_ref, shard_ref, *refs, heads, count, base, steps, ahead, q_views):
    given, (out_ref, win_ref, held_ref, mixed_ref, kv_sems, q_sems, out_sems) = refs[:-7], refs[-7:]
    width = heads * HD
    own_ref = given[0]

    def copy_own():
        rows = (base + steps) * BLK
        return pltpu.make_async_copy(
            own_ref.at[pl.ds(0, rows), pl.ds(0, 2 * HD)], win_ref.at[pl.ds(ahead * BLK, rows)], kv_sems.at[0]
        )

    def copy_halo():
        return pltpu.make_async_copy(given[1], win_ref.at[pl.ds(0, ahead * BLK)], kv_sems.at[1])

    def copy_out(step):
        return pltpu.make_async_copy(
            mixed_ref.at[step], out_ref.at[slot_ref[base + step]], out_sems.at[step]
        )

    copy_own().start()
    if ahead:
        copy_halo().start()
    for view in range(steps):
        which, lead, row, column = q_views[view]
        source = given[which] if lead is None else given[which].at[lead]
        step = order_ref[view]
        pltpu.make_async_copy(
            source.at[pl.ds(row, BLK), pl.ds(column, width)], held_ref.at[step], q_sems.at[step]
        ).start()

    row = lax.broadcasted_iota(jnp.int32, (BLK, BLK), 0)
    column = lax.broadcasted_iota(jnp.int32, (BLK, BLK), 1)
    causal = column <= row
    copy_own().wait()
    if ahead:
        copy_halo().wait()

    def per_block(step, _):
        index = base + step
        block = shard_ref[0] * count + index
        doc = doc_ref[block]
        tiles = jnp.int32(1)
        for back in range(1, MAXDOC):
            at = jnp.maximum(block - back, 0)
            tiles += jnp.where((block >= back) & (doc_ref[at] == doc), 1, 0)
        pltpu.make_async_copy(held_ref.at[step], held_ref.at[step], q_sems.at[step]).wait()

        def with_tiles(n):
            start = pl.multiple_of((index + ahead + 1 - n) * BLK, BLK)
            keys = win_ref[pl.ds(start, n * BLK), :HD]
            values = win_ref[pl.ds(start, n * BLK), HD:]
            for head in range(heads):
                columns = slice(head * HD, (head + 1) * HD)
                scores = lax.dot_general(
                    held_ref[step, :, columns],
                    keys,
                    (((1,), (1,)), ((), ())),
                    preferred_element_type=jnp.float32,
                )
                last = jnp.where(causal, scores[:, (n - 1) * BLK :], -jnp.inf)
                if n > 1:
                    scores = jnp.concatenate([scores[:, : (n - 1) * BLK], last], axis=1)
                else:
                    scores = last
                top = jnp.max(scores, axis=1, keepdims=True)
                expo = jnp.exp2((scores - top) * EXP2_SCALE)
                total = jnp.sum(expo, axis=1, keepdims=True)
                mixed = jnp.dot(expo.astype(jnp.bfloat16), values, preferred_element_type=jnp.float32)
                mixed_ref[step, :, columns] = (mixed / total).astype(jnp.bfloat16)

        for n in range(1, MAXDOC + 1):
            pl.when(tiles == n)(functools.partial(with_tiles, n))
        copy_out(step).start()
        return 0

    lax.fori_loop(0, steps, per_block, 0)
    for step in range(steps):
        copy_out(step).wait()


def attend(own, halo, sources, q_views, order, heads, tables, count, slots, base=0, steps=None, result=None):
    doc_ids, slot, shard = tables
    steps = count if steps is None else steps
    width = heads * HD
    ahead = 0 if halo is None else HALO
    given = [own] + ([] if halo is None else [halo])
    views = [(len(given) + which if which >= 0 else 0, lead, row, column) for which, lead, row, column in q_views]
    given = given + list(sources) + ([] if result is None else [result])
    smem, anywhere = pl.BlockSpec(memory_space=pltpu.SMEM), pl.BlockSpec(memory_space=pl.ANY)
    return pl.pallas_call(
        functools.partial(
            attend_kernel, heads=heads, count=count, base=base, steps=steps, ahead=ahead, q_views=views
        ),
        in_specs=[smem] * 4 + [anywhere] * len(given),
        out_specs=pl.BlockSpec(memory_space=pl.ANY),
        out_shape=jax.ShapeDtypeStruct((slots, BLK, width), jnp.bfloat16),
        scratch_shapes=[
            pltpu.VMEM(((base + steps + ahead) * BLK, 2 * HD), jnp.bfloat16),
            pltpu.VMEM((steps, BLK, width), jnp.bfloat16),
            pltpu.VMEM((steps, BLK, width), jnp.bfloat16),
            pltpu.SemaphoreType.DMA((2,)),
            pltpu.SemaphoreType.DMA((steps,)),
            pltpu.SemaphoreType.DMA((steps,)),
        ],
        input_output_aliases={} if result is None else {4 + len(given) - 1: 0},
        compiler_params=pltpu.CompilerParams(vmem_limit_bytes=VMEM_BYTES),
        cost_estimate=pl.CostEstimate(
            flops=4 * steps * BLK * heads * HD * BLK * 4,
            bytes_accessed=4 * steps * BLK * width + 4 * (base + steps) * BLK * HD,
            transcendentals=steps * BLK * heads * BLK * 4,
        ),
        name="attend",
    )(doc_ids, slot, order, shard, *given)


def first_parts_kernel(k_ref, v_ref, q_ref, out_ref, held_ref, in_sems, out_sems, *, head_count, width):
    kv_width, q_width = k_ref.shape[1] // head_count, q_ref.shape[1] // head_count
    rows = q_ref.shape[0]

    def fetches(h):
        pieces = (
            (k_ref, h * kv_width, 0, kv_width),
            (v_ref, h * kv_width, kv_width, kv_width),
            (q_ref, h * q_width, 2 * kv_width, width),
        )
        return [
            pltpu.make_async_copy(
                ref.at[:, pl.ds(at, size)], held_ref.at[h, :, pl.ds(to, size)], in_sems.at[h, i]
            )
            for i, (ref, at, to, size) in enumerate(pieces)
        ]

    def store(h):
        return pltpu.make_async_copy(held_ref.at[h], out_ref.at[h], out_sems.at[h])

    for h in range(head_count):
        for fetch in fetches(h):
            fetch.start()
    for h in range(head_count):
        for fetch in fetches(h):
            fetch.wait()
        store(h).start()
    for h in range(head_count):
        store(h).wait()


def first_parts(key, value, query, head_count, width):
    shape = (head_count, query.shape[0], 2 * key.shape[1] // head_count + width)
    return pl.pallas_call(
        functools.partial(first_parts_kernel, head_count=head_count, width=width),
        in_specs=[pl.BlockSpec(memory_space=pl.ANY)] * 3,
        out_specs=pl.BlockSpec(memory_space=pl.ANY),
        out_shape=jax.ShapeDtypeStruct(shape, jnp.bfloat16),
        scratch_shapes=[
            pltpu.VMEM(shape, jnp.bfloat16),
            pltpu.SemaphoreType.DMA((head_count, 3)),
            pltpu.SemaphoreType.DMA((head_count,)),
        ],
        compiler_params=pltpu.CompilerParams(vmem_limit_bytes=VMEM_BYTES),
        name="first_parts",
    )(key, value, query)


def later_parts_kernel(place_ref, q_ref, *refs, chips, firsts, widths):
    sems, held_refs, out_refs = refs[-2:], refs[-2 - len(widths) : -2], refs[: -2 - len(widths)]
    core, chip = place_ref[0], place_ref[1]
    q_width = q_ref.shape[1] // (2 * chips)
    moves = []
    for chunk, (first, width) in enumerate(zip(firsts, widths)):
        for side in range(2):
            for step in range(chips):
                member = lax.rem(chip + step, chips) * 2 + lax.rem(core + side, 2)
                column = pl.multiple_of(member * q_width + first, HD)
                held = held_refs[chunk].at[side * chips + step]
                at = (chunk * 2 + side) * chips + step
                moves.append((
                    pltpu.make_async_copy(q_ref.at[:, pl.ds(column, width)], held, sems[0].at[at]),
                    pltpu.make_async_copy(held, out_refs[at], sems[1].at[at]),
                ))
    for fetch, _ in moves:
        fetch.start()
    for fetch, store in moves:
        fetch.wait()
        store.start()
    for _, store in moves:
        store.wait()


def later_parts(query, place, head_count, firsts, widths):
    rows, chips = query.shape[0], head_count // 2
    shapes = [jax.ShapeDtypeStruct((rows, width), jnp.bfloat16) for width in widths for _ in range(2 * chips)]
    outs = pl.pallas_call(
        functools.partial(later_parts_kernel, chips=chips, firsts=firsts, widths=widths),
        in_specs=[pl.BlockSpec(memory_space=pltpu.SMEM), pl.BlockSpec(memory_space=pl.ANY)],
        out_specs=[pl.BlockSpec(memory_space=pl.ANY)] * len(shapes),
        out_shape=shapes,
        scratch_shapes=[pltpu.VMEM((2 * chips, rows, width), jnp.bfloat16) for width in widths]
        + [pltpu.SemaphoreType.DMA((len(shapes),))] * 2,
        compiler_params=pltpu.CompilerParams(vmem_limit_bytes=VMEM_BYTES),
        cost_estimate=pl.CostEstimate(flops=0, bytes_accessed=4 * query.size, transcendentals=0),
        name="later_parts",
    )(place, query)
    kept = [list(outs[2 * chips * i : 2 * chips * i + chips]) for i in range(len(widths))]
    given = [list(outs[2 * chips * i + chips : 2 * chips * (i + 1)]) for i in range(len(widths))]
    return kept, given


def place_kernel(source_ref, *refs, count, first, width):
    received_ref, out_ref, held_ref, in_sems, out_sems = refs[0], refs[-4], refs[-3], refs[-2], refs[-1]

    def fetch(i):
        return pltpu.make_async_copy(received_ref.at[source_ref[i]], held_ref.at[i], in_sems.at[i])

    def store(i):
        return pltpu.make_async_copy(
            held_ref.at[i], out_ref.at[pl.ds(i * BLK, BLK), pl.ds(first, width)], out_sems.at[i]
        )

    for i in range(count):
        fetch(i).start()
    for i in range(count):
        fetch(i).wait()
        store(i).start()
    for i in range(count):
        store(i).wait()


def place(received, source, result, first, count, full_width):
    slots, _, width = received.shape
    given = [received] if result is None else [received, result]
    return pl.pallas_call(
        functools.partial(place_kernel, count=count, first=first, width=width),
        in_specs=[pl.BlockSpec(memory_space=pltpu.SMEM)] + [pl.BlockSpec(memory_space=pl.ANY)] * len(given),
        out_specs=pl.BlockSpec(memory_space=pl.ANY),
        out_shape=jax.ShapeDtypeStruct((count * BLK, full_width), jnp.bfloat16),
        scratch_shapes=[
            pltpu.VMEM((count, BLK, width), jnp.bfloat16),
            pltpu.SemaphoreType.DMA((count,)),
            pltpu.SemaphoreType.DMA((count,)),
        ],
        input_output_aliases={} if result is None else {2: 0},
        compiler_params=pltpu.CompilerParams(vmem_limit_bytes=VMEM_BYTES),
        cost_estimate=pl.CostEstimate(flops=0, bytes_accessed=4 * count * BLK * width, transcendentals=0),
        name="place",
    )(source, *given)


def shards(query, key, value, doc_ids, plan):
    head_count = lax.axis_size("head")
    shard_count = lax.axis_size("ctx")
    local_rows = query.shape[0]
    rows = head_count * local_rows
    count = rows // BLK
    per_device = local_rows // BLK
    q_width = query.shape[1] // head_count
    shard = lax.axis_index("ctx").astype(jnp.int32)
    member = lax.axis_index("head").astype(jnp.int32)
    core, chip, chips = member % 2, member // 2, head_count // 2

    widths = [heads * HD for heads in CHUNKS]
    firsts = [sum(widths[:i]) for i in range(len(widths))]
    opening = first_parts(key, value, query, head_count, widths[0])
    kept, given = later_parts(query, jnp.stack([core, chip]), head_count, firsts[1:], widths[1:])
    swap = [(h, h ^ 1) for h in range(head_count)]
    got = [[lax.ppermute(part, "head", swap) for part in parts] for parts in given]
    opening = lax.all_to_all(opening, "head", split_axis=0, concat_axis=0, tiled=True)

    index = jnp.arange(count, dtype=jnp.int32)
    own_ids = shard * count + index
    position = jnp.arange(plan.shape[0], dtype=jnp.int32)
    target = jnp.sum(
        jnp.where(plan[None, :] == own_ids[:, None], position[None, :] // count, 0), axis=1, dtype=jnp.int32
    )
    source = lax.dynamic_slice_in_dim(plan, shard * count, count) // count
    step_of, rest = index // (2 * per_device), index % (2 * per_device)
    giver = (chip - step_of + chips) % chips * 2 + (core + rest // per_device) % 2
    arrival = giver * per_device + rest % per_device

    opening, kept, got, target, source, arrival = lax.optimization_barrier(
        (opening, kept, got, target, source, arrival)
    )
    opening = opening.reshape(rows, 2 * HD + widths[0])
    halo = lax.ppermute(
        opening[rows - HALO * BLK :, : 2 * HD], "ctx", [(i, i + 1) for i in range(shard_count - 1)]
    )
    tables = (doc_ids, target, shard.reshape(1))

    result = None
    for turn, heads in enumerate(CHUNKS):
        if turn == 0:
            views = [(-1, None, i * BLK, 2 * HD) for i in range(count)]
            sent = attend(
                opening, None, [], views[HALO:], index, heads, tables, count, shard_count, HALO, count - HALO
            )
            sent = attend(
                opening, halo, [], views[:HALO], index, heads, tables, count, shard_count, 0, HALO, sent
            )
        else:
            sources = []
            for step in range(chips):
                onward = [(h, (h + 2 * step) % head_count) for h in range(head_count)]
                for part in (kept[turn - 1][step], got[turn - 1][step]):
                    sources.append(lax.ppermute(part, "head", onward) if step else part)
            views = [(i // per_device, None, i % per_device * BLK, 0) for i in range(count)]
            sent = attend(opening, halo, sources, views, arrival, heads, tables, count, shard_count)
        received = lax.all_to_all(sent, "ctx", split_axis=0, concat_axis=0, tiled=True)
        result = place(received, source, result, firsts[turn], count, q_width)
    return result


def solution(mesh):
    return jax.shard_map(
        shards,
        mesh=mesh,
        in_specs=(
            P(("ctx", "head"), None),
            P(("ctx", "head"), None),
            P(("ctx", "head"), None),
            P(),
            P(),
        ),
        out_specs=P("ctx", "head"),
        check_vma=False,
    )
```

```python
import functools
import math

import jax
import jax.numpy as jnp
from jax import lax
from jax.experimental import pallas as pl
from jax.experimental.pallas import tpu as pltpu
from jax.sharding import PartitionSpec as P

HD = 128
BLK = 128
MAXDOC = 8
VMEM_BYTES = 60 * 1024 * 1024
SHARED_VMEM_BYTES = 32 * 1024 * 1024
HALO = MAXDOC - 1
CHUNKS = (2, 6)
EXP2_SCALE = math.log2(math.e) / math.sqrt(HD)


def attend_kernel(doc_ref, slot_ref, order_ref, shard_ref, *refs, heads, count, base, steps, ahead, q_views):
    given, (out_ref, win_ref, held_ref, mixed_ref, kv_sems, q_sems, out_sems) = refs[:-7], refs[-7:]
    width = heads * HD
    own_ref = given[0]

    def copy_own():
        rows = (base + steps) * BLK
        return pltpu.make_async_copy(
            own_ref.at[pl.ds(0, rows), pl.ds(0, 2 * HD)], win_ref.at[pl.ds(ahead * BLK, rows)], kv_sems.at[0]
        )

    def copy_halo():
        return pltpu.make_async_copy(given[1], win_ref.at[pl.ds(0, ahead * BLK)], kv_sems.at[1])

    def copy_out(step):
        return pltpu.make_async_copy(
            mixed_ref.at[step], out_ref.at[slot_ref[base + step]], out_sems.at[step]
        )

    copy_own().start()
    if ahead:
        copy_halo().start()
    for view in range(steps):
        which, lead, row, column = q_views[view]
        source = given[which] if lead is None else given[which].at[lead]
        step = order_ref[view]
        pltpu.make_async_copy(
            source.at[pl.ds(row, BLK), pl.ds(column, width)], held_ref.at[step], q_sems.at[step]
        ).start()

    row = lax.broadcasted_iota(jnp.int32, (heads * BLK, BLK), 0) % BLK
    column = lax.broadcasted_iota(jnp.int32, (heads * BLK, BLK), 1)
    causal = column <= row
    copy_own().wait()
    if ahead:
        copy_halo().wait()

    def per_pair(pair, _):
        at = 2 * pair
        first = base + at
        block = shard_ref[0] * count + first
        doc = doc_ref[block]
        tiles = jnp.int32(1)
        for back in range(1, MAXDOC):
            before = jnp.maximum(block - back, 0)
            tiles += jnp.where((block >= back) & (doc_ref[before] == doc), 1, 0)
        same = doc_ref[block + 1] == doc
        for lane in range(2):
            held = held_ref.at[at + lane]
            pltpu.make_async_copy(held, held, q_sems.at[at + lane]).wait()

        def with_tiles(tiles_of):
            windows = []
            for lane, n in enumerate(tiles_of):
                start = pl.multiple_of((first + lane + ahead + 1 - n) * BLK, BLK)
                windows.append(pl.ds(start, n * BLK))
            scores = []
            for lane, n in enumerate(tiles_of):
                queries = jnp.concatenate(
                    [held_ref[at + lane, :, head * HD : (head + 1) * HD] for head in range(heads)], axis=0
                )
                scores.append(lax.dot_general(
                    queries, win_ref[windows[lane], :HD], (((1,), (1,)), ((), ())),
                    preferred_element_type=jnp.float32,
                ))
            for lane, n in enumerate(tiles_of):
                last = jnp.where(causal, scores[lane][:, (n - 1) * BLK :], -jnp.inf)
                scores[lane] = (
                    last if n == 1 else jnp.concatenate([scores[lane][:, : (n - 1) * BLK], last], axis=1)
                )
            tops = [jnp.max(s, axis=1, keepdims=True) for s in scores]
            expos = [jnp.exp2((s - top) * EXP2_SCALE) for s, top in zip(scores, tops)]
            totals = [jnp.sum(e, axis=1, keepdims=True) for e in expos]
            sums = [
                jnp.dot(e.astype(jnp.bfloat16), win_ref[window, HD:], preferred_element_type=jnp.float32)
                for e, window in zip(expos, windows)
            ]
            for lane in range(len(tiles_of)):
                mixed = (sums[lane] / totals[lane]).astype(jnp.bfloat16)
                for head in range(heads):
                    mixed_ref[at + lane, :, head * HD : (head + 1) * HD] = mixed[head * BLK : (head + 1) * BLK]

        for n in range(1, MAXDOC + 1):
            if n < MAXDOC:
                pl.when((tiles == n) & same)(functools.partial(with_tiles, (n, n + 1)))
            pl.when((tiles == n) & jnp.logical_not(same))(functools.partial(with_tiles, (n, 1)))
        copy_out(at).start()
        copy_out(at + 1).start()
        return 0

    lax.fori_loop(0, steps // 2, per_pair, 0)
    for step in range(steps):
        copy_out(step).wait()


def attend(own, halo, sources, q_views, order, heads, tables, count, slots, base=0, steps=None, result=None):
    doc_ids, slot, shard = tables
    steps = count if steps is None else steps
    width = heads * HD
    ahead = 0 if halo is None else HALO
    alone = steps < count
    given = [own] + ([] if halo is None else [halo])
    views = [(len(given) + which if which >= 0 else 0, lead, row, column) for which, lead, row, column in q_views]
    given = given + list(sources) + ([] if result is None else [result])
    smem, anywhere = pl.BlockSpec(memory_space=pltpu.SMEM), pl.BlockSpec(memory_space=pl.ANY)
    return pl.pallas_call(
        functools.partial(
            attend_kernel, heads=heads, count=count, base=base, steps=steps, ahead=ahead, q_views=views
        ),
        in_specs=[smem] * 4 + [anywhere] * len(given),
        out_specs=pl.BlockSpec(memory_space=pl.ANY),
        out_shape=jax.ShapeDtypeStruct((slots, BLK, width), jnp.bfloat16),
        scratch_shapes=[
            pltpu.VMEM(((base + steps + ahead) * BLK, 2 * HD), jnp.bfloat16),
            pltpu.VMEM((steps, BLK, width), jnp.bfloat16),
            pltpu.VMEM((steps, BLK, width), jnp.bfloat16),
            pltpu.SemaphoreType.DMA((2,)),
            pltpu.SemaphoreType.DMA((steps,)),
            pltpu.SemaphoreType.DMA((steps,)),
        ],
        input_output_aliases={} if result is None else {4 + len(given) - 1: 0},
        compiler_params=pltpu.CompilerParams(vmem_limit_bytes=VMEM_BYTES if alone else SHARED_VMEM_BYTES),
        cost_estimate=pl.CostEstimate(flops=0 if alone else 10**12, bytes_accessed=0, transcendentals=0),
        name="attend",
    )(doc_ids, slot, order, shard, *given)


def first_parts_kernel(k_ref, v_ref, q_ref, out_ref, held_ref, in_sems, out_sems, *, head_count, width):
    kv_width, q_width = k_ref.shape[1] // head_count, q_ref.shape[1] // head_count
    rows = q_ref.shape[0]

    def fetches(h):
        pieces = (
            (k_ref, h * kv_width, 0, kv_width),
            (v_ref, h * kv_width, kv_width, kv_width),
            (q_ref, h * q_width, 2 * kv_width, width),
        )
        return [
            pltpu.make_async_copy(
                ref.at[:, pl.ds(at, size)], held_ref.at[h, :, pl.ds(to, size)], in_sems.at[h, i]
            )
            for i, (ref, at, to, size) in enumerate(pieces)
        ]

    def store(h):
        return pltpu.make_async_copy(held_ref.at[h], out_ref.at[h], out_sems.at[h])

    for h in range(head_count):
        for fetch in fetches(h):
            fetch.start()
    for h in range(head_count):
        for fetch in fetches(h):
            fetch.wait()
        store(h).start()
    for h in range(head_count):
        store(h).wait()


def first_parts(key, value, query, head_count, width):
    shape = (head_count, query.shape[0], 2 * key.shape[1] // head_count + width)
    return pl.pallas_call(
        functools.partial(first_parts_kernel, head_count=head_count, width=width),
        in_specs=[pl.BlockSpec(memory_space=pl.ANY)] * 3,
        out_specs=pl.BlockSpec(memory_space=pl.ANY),
        out_shape=jax.ShapeDtypeStruct(shape, jnp.bfloat16),
        scratch_shapes=[
            pltpu.VMEM(shape, jnp.bfloat16),
            pltpu.SemaphoreType.DMA((head_count, 3)),
            pltpu.SemaphoreType.DMA((head_count,)),
        ],
        compiler_params=pltpu.CompilerParams(vmem_limit_bytes=VMEM_BYTES),
        name="first_parts",
    )(key, value, query)


def later_parts_kernel(place_ref, q_ref, *refs, chips, firsts, widths):
    chunks = len(widths)
    in_sems, out_sems = refs[-2:]
    held_refs, out_refs = refs[-2 - chunks : -2], refs[: -2 - chunks]
    core, chip = place_ref[0], place_ref[1]
    q_width = q_ref.shape[1] // (2 * chips)
    moves = []
    for chunk, (first, width) in enumerate(zip(firsts, widths)):
        outs = out_refs[chunk * (chips + 1) : (chunk + 1) * (chips + 1)]
        for side in range(2):
            for step in range(chips):
                member = lax.rem(chip + step, chips) * 2 + lax.rem(core + side, 2)
                column = pl.multiple_of(member * q_width + first, HD)
                held = held_refs[chunk].at[side * chips + step]
                at = (chunk * 2 + side) * chips + step
                out = outs[chips].at[step] if side else outs[step].at[0]
                moves.append((
                    pltpu.make_async_copy(q_ref.at[:, pl.ds(column, width)], held, in_sems.at[at]),
                    pltpu.make_async_copy(held, out, out_sems.at[at]),
                ))
    for fetch, _ in moves:
        fetch.start()
    for fetch, store in moves:
        fetch.wait()
        store.start()
    for _, store in moves:
        store.wait()


def later_parts(query, place, head_count, firsts, widths):
    rows, chips = query.shape[0], head_count // 2
    shapes = []
    for width in widths:
        shapes += [jax.ShapeDtypeStruct((2, rows, width), jnp.bfloat16)] * chips
        shapes.append(jax.ShapeDtypeStruct((chips, rows, width), jnp.bfloat16))
    copies = 2 * chips * len(widths)
    outs = pl.pallas_call(
        functools.partial(later_parts_kernel, chips=chips, firsts=firsts, widths=widths),
        in_specs=[pl.BlockSpec(memory_space=pltpu.SMEM), pl.BlockSpec(memory_space=pl.ANY)],
        out_specs=[pl.BlockSpec(memory_space=pl.ANY)] * len(shapes),
        out_shape=shapes,
        scratch_shapes=[pltpu.VMEM((2 * chips, rows, width), jnp.bfloat16) for width in widths]
        + [pltpu.SemaphoreType.DMA((copies,))] * 2,
        compiler_params=pltpu.CompilerParams(vmem_limit_bytes=VMEM_BYTES),
        cost_estimate=pl.CostEstimate(flops=0, bytes_accessed=4 * query.size, transcendentals=0),
        name="later_parts",
    )(place, query)
    split = [outs[(chips + 1) * i : (chips + 1) * (i + 1)] for i in range(len(widths))]
    return [list(part[:chips]) for part in split], [part[chips] for part in split]


def fill_kernel(got_ref, *refs):
    held_ref, in_sems, out_sems = refs[-3:]
    steps = held_ref.shape[0]
    out_refs = refs[steps : 2 * steps]
    fetches = [pltpu.make_async_copy(got_ref.at[i], held_ref.at[i], in_sems.at[i]) for i in range(steps)]
    stores = [pltpu.make_async_copy(held_ref.at[i], out_refs[i].at[1], out_sems.at[i]) for i in range(steps)]
    for fetch in fetches:
        fetch.start()
    for fetch, store in zip(fetches, stores):
        fetch.wait()
        store.start()
    for store in stores:
        store.wait()


def fill(parts, got):
    return pl.pallas_call(
        fill_kernel,
        in_specs=[pl.BlockSpec(memory_space=pl.ANY)] * (1 + len(parts)),
        out_specs=[pl.BlockSpec(memory_space=pl.ANY)] * len(parts),
        out_shape=[jax.ShapeDtypeStruct(part.shape, part.dtype) for part in parts],
        scratch_shapes=[pltpu.VMEM(got.shape, got.dtype)] + [pltpu.SemaphoreType.DMA((len(parts),))] * 2,
        input_output_aliases={1 + i: i for i in range(len(parts))},
        compiler_params=pltpu.CompilerParams(vmem_limit_bytes=VMEM_BYTES),
        cost_estimate=pl.CostEstimate(flops=0, bytes_accessed=0, transcendentals=0),
        name="fill",
    )(got, *parts)


def place_kernel(source_ref, *refs, count, first, width):
    received_ref, out_ref, held_ref, in_sems, out_sems = refs[0], refs[-4], refs[-3], refs[-2], refs[-1]

    def fetch(i):
        return pltpu.make_async_copy(received_ref.at[source_ref[i]], held_ref.at[i], in_sems.at[i])

    def store(i):
        return pltpu.make_async_copy(
            held_ref.at[i], out_ref.at[pl.ds(i * BLK, BLK), pl.ds(first, width)], out_sems.at[i]
        )

    for i in range(count):
        fetch(i).start()
    for i in range(count):
        fetch(i).wait()
        store(i).start()
    for i in range(count):
        store(i).wait()


def place(received, source, result, first, count, full_width):
    slots, _, width = received.shape
    given = [received] if result is None else [received, result]
    return pl.pallas_call(
        functools.partial(place_kernel, count=count, first=first, width=width),
        in_specs=[pl.BlockSpec(memory_space=pltpu.SMEM)] + [pl.BlockSpec(memory_space=pl.ANY)] * len(given),
        out_specs=pl.BlockSpec(memory_space=pl.ANY),
        out_shape=jax.ShapeDtypeStruct((count * BLK, full_width), jnp.bfloat16),
        scratch_shapes=[
            pltpu.VMEM((count, BLK, width), jnp.bfloat16),
            pltpu.SemaphoreType.DMA((count,)),
            pltpu.SemaphoreType.DMA((count,)),
        ],
        input_output_aliases={} if result is None else {2: 0},
        compiler_params=pltpu.CompilerParams(vmem_limit_bytes=SHARED_VMEM_BYTES),
        cost_estimate=pl.CostEstimate(flops=0, bytes_accessed=4 * count * BLK * width, transcendentals=0),
        name="place",
    )(source, *given)


def shards(query, key, value, doc_ids, plan):
    head_count = lax.axis_size("head")
    shard_count = lax.axis_size("ctx")
    local_rows = query.shape[0]
    rows = head_count * local_rows
    count = rows // BLK
    per_device = local_rows // BLK
    q_width = query.shape[1] // head_count
    shard = lax.axis_index("ctx").astype(jnp.int32)
    member = lax.axis_index("head").astype(jnp.int32)
    core, chip, chips = member % 2, member // 2, head_count // 2

    widths = [heads * HD for heads in CHUNKS]
    firsts = [sum(widths[:i]) for i in range(len(widths))]
    opening = first_parts(key, value, query, head_count, widths[0])
    kept, given = later_parts(query, jnp.stack([core, chip]), head_count, firsts[1:], widths[1:])
    swap = [(h, h ^ 1) for h in range(head_count)]
    later = [fill(parts, lax.ppermute(part, "head", swap)) for parts, part in zip(kept, given)]
    opening = lax.all_to_all(opening, "head", split_axis=0, concat_axis=0, tiled=True)

    index = jnp.arange(count, dtype=jnp.int32)
    own_ids = shard * count + index
    position = jnp.arange(plan.shape[0], dtype=jnp.int32)
    target = jnp.sum(
        jnp.where(plan[None, :] == own_ids[:, None], position[None, :] // count, 0), axis=1, dtype=jnp.int32
    )
    source = lax.dynamic_slice_in_dim(plan, shard * count, count) // count
    step_of, rest = index // (2 * per_device), index % (2 * per_device)
    giver = (chip - step_of + chips) % chips * 2 + (core + rest // per_device) % 2
    arrival = giver * per_device + rest % per_device

    opening, later, target, source, arrival = lax.optimization_barrier(
        (opening, later, target, source, arrival)
    )
    opening = opening.reshape(rows, 2 * HD + widths[0])
    halo = lax.ppermute(
        opening[rows - HALO * BLK :, : 2 * HD], "ctx", [(i, i + 1) for i in range(shard_count - 1)]
    )
    tables = (doc_ids, target, shard.reshape(1))

    result = None
    for turn, heads in enumerate(CHUNKS):
        if turn == 0:
            views = [(-1, None, i * BLK, 2 * HD) for i in range(count)]
            sent = attend(
                opening, None, [], views[MAXDOC:], index, heads, tables, count, shard_count, MAXDOC, count - MAXDOC
            )
            sent = attend(
                opening, halo, [], views[:MAXDOC], index, heads, tables, count, shard_count, 0, MAXDOC, sent
            )
        else:
            sources = []
            for step, part in enumerate(later[turn - 1]):
                onward = [(h, (h + 2 * step) % head_count) for h in range(head_count)]
                sources.append(lax.ppermute(part, "head", onward) if step else part)
            views = [
                (i // (2 * per_device), i // per_device % 2, i % per_device * BLK, 0) for i in range(count)
            ]
            sent = attend(opening, halo, sources, views, arrival, heads, tables, count, shard_count)
        received = lax.all_to_all(sent, "ctx", split_axis=0, concat_axis=0, tiled=True)
        result = place(received, source, result, firsts[turn], count, q_width)
    return result


def solution(mesh):
    return jax.shard_map(
        shards,
        mesh=mesh,
        in_specs=(
            P(("ctx", "head"), None),
            P(("ctx", "head"), None),
            P(("ctx", "head"), None),
            P(),
            P(),
        ),
        out_specs=P("ctx", "head"),
        check_vma=False,
    )
```

```python
import functools
import math

import jax
import jax.numpy as jnp
from jax import lax
from jax.experimental import pallas as pl
from jax.experimental.pallas import tpu as pltpu
from jax.sharding import PartitionSpec as P

HD = 128
BLK = 128
MAXDOC = 8
VMEM_BYTES = 60 * 1024 * 1024
SHARED_VMEM_BYTES = 32 * 1024 * 1024
HALO = MAXDOC - 1
CHUNKS = (2, 6)
EXP2_SCALE = math.log2(math.e) / math.sqrt(HD)


def attend_kernel(doc_ref, slot_ref, order_ref, shard_ref, *refs, heads, count, base, steps, ahead, q_views):
    given, (out_ref, win_ref, held_ref, mixed_ref, kv_sems, q_sems, out_sems) = refs[:-7], refs[-7:]
    width = heads * HD
    own_ref = given[0]

    def copy_own():
        rows = (base + steps) * BLK
        return pltpu.make_async_copy(
            own_ref.at[pl.ds(0, rows), pl.ds(0, 2 * HD)], win_ref.at[pl.ds(ahead * BLK, rows)], kv_sems.at[0]
        )

    def copy_halo():
        return pltpu.make_async_copy(given[1], win_ref.at[pl.ds(0, ahead * BLK)], kv_sems.at[1])

    def copy_out(step):
        return pltpu.make_async_copy(
            mixed_ref.at[step], out_ref.at[slot_ref[base + step]], out_sems.at[step]
        )

    copy_own().start()
    if ahead:
        copy_halo().start()
    for view in range(steps):
        which, lead, row, column = q_views[view]
        source = given[which] if lead is None else given[which].at[lead]
        step = order_ref[view]
        pltpu.make_async_copy(
            source.at[pl.ds(row, BLK), pl.ds(column, width)], held_ref.at[step], q_sems.at[step]
        ).start()

    row = lax.broadcasted_iota(jnp.int32, (heads * BLK, BLK), 0) % BLK
    column = lax.broadcasted_iota(jnp.int32, (heads * BLK, BLK), 1)
    causal = column <= row
    copy_own().wait()
    if ahead:
        copy_halo().wait()

    def per_pair(pair, _):
        at = 2 * pair
        first = base + at
        block = shard_ref[0] * count + first
        doc = doc_ref[block]
        tiles = jnp.int32(1)
        for back in range(1, MAXDOC):
            before = jnp.maximum(block - back, 0)
            tiles += jnp.where((block >= back) & (doc_ref[before] == doc), 1, 0)
        same = doc_ref[block + 1] == doc
        for lane in range(2):
            held = held_ref.at[at + lane]
            pltpu.make_async_copy(held, held, q_sems.at[at + lane]).wait()

        def with_tiles(tiles_of):
            windows = []
            for lane, n in enumerate(tiles_of):
                start = pl.multiple_of((first + lane + ahead + 1 - n) * BLK, BLK)
                windows.append(pl.ds(start, n * BLK))
            scores = []
            for lane, n in enumerate(tiles_of):
                queries = jnp.concatenate(
                    [held_ref[at + lane, :, head * HD : (head + 1) * HD] for head in range(heads)], axis=0
                )
                scores.append(lax.dot_general(
                    queries, win_ref[windows[lane], :HD], (((1,), (1,)), ((), ())),
                    preferred_element_type=jnp.float32,
                ))
            for lane, n in enumerate(tiles_of):
                last = jnp.where(causal, scores[lane][:, (n - 1) * BLK :], -jnp.inf)
                scores[lane] = (
                    last if n == 1 else jnp.concatenate([scores[lane][:, : (n - 1) * BLK], last], axis=1)
                )
            tops = [jnp.max(s, axis=1, keepdims=True) for s in scores]
            expos = [jnp.exp2((s - top) * EXP2_SCALE) for s, top in zip(scores, tops)]
            totals = [jnp.sum(e, axis=1, keepdims=True) for e in expos]
            sums = [
                jnp.dot(e.astype(jnp.bfloat16), win_ref[window, HD:], preferred_element_type=jnp.float32)
                for e, window in zip(expos, windows)
            ]
            for lane in range(len(tiles_of)):
                mixed = (sums[lane] / totals[lane]).astype(jnp.bfloat16)
                for head in range(heads):
                    mixed_ref[at + lane, :, head * HD : (head + 1) * HD] = mixed[head * BLK : (head + 1) * BLK]

        for n in range(1, MAXDOC + 1):
            if n < MAXDOC:
                pl.when((tiles == n) & same)(functools.partial(with_tiles, (n, n + 1)))
            pl.when((tiles == n) & jnp.logical_not(same))(functools.partial(with_tiles, (n, 1)))
        copy_out(at).start()
        copy_out(at + 1).start()
        return 0

    lax.fori_loop(0, steps // 2, per_pair, 0)
    for step in range(steps):
        copy_out(step).wait()


def attend(own, halo, sources, q_views, order, heads, tables, count, slots, base=0, steps=None, result=None):
    doc_ids, slot, shard = tables
    steps = count if steps is None else steps
    width = heads * HD
    ahead = 0 if halo is None else HALO
    alone = steps < count
    given = [own] + ([] if halo is None else [halo])
    views = [(len(given) + which if which >= 0 else 0, lead, row, column) for which, lead, row, column in q_views]
    given = given + list(sources) + ([] if result is None else [result])
    smem, anywhere = pl.BlockSpec(memory_space=pltpu.SMEM), pl.BlockSpec(memory_space=pl.ANY)
    return pl.pallas_call(
        functools.partial(
            attend_kernel, heads=heads, count=count, base=base, steps=steps, ahead=ahead, q_views=views
        ),
        in_specs=[smem] * 4 + [anywhere] * len(given),
        out_specs=pl.BlockSpec(memory_space=pl.ANY),
        out_shape=jax.ShapeDtypeStruct((slots, BLK, width), jnp.bfloat16),
        scratch_shapes=[
            pltpu.VMEM(((base + steps + ahead) * BLK, 2 * HD), jnp.bfloat16),
            pltpu.VMEM((steps, BLK, width), jnp.bfloat16),
            pltpu.VMEM((steps, BLK, width), jnp.bfloat16),
            pltpu.SemaphoreType.DMA((2,)),
            pltpu.SemaphoreType.DMA((steps,)),
            pltpu.SemaphoreType.DMA((steps,)),
        ],
        input_output_aliases={} if result is None else {4 + len(given) - 1: 0},
        compiler_params=pltpu.CompilerParams(vmem_limit_bytes=VMEM_BYTES if alone else SHARED_VMEM_BYTES),
        cost_estimate=pl.CostEstimate(
            flops=10**12 if ahead else 0, bytes_accessed=0, transcendentals=0
        ),
        name="attend",
    )(doc_ids, slot, order, shard, *given)


def first_parts_kernel(k_ref, v_ref, q_ref, out_ref, held_ref, in_sems, out_sems, *, head_count, width):
    kv_width, q_width = k_ref.shape[1] // head_count, q_ref.shape[1] // head_count
    rows = q_ref.shape[0]

    def fetches(h):
        pieces = (
            (k_ref, h * kv_width, 0, kv_width),
            (v_ref, h * kv_width, kv_width, kv_width),
            (q_ref, h * q_width, 2 * kv_width, width),
        )
        return [
            pltpu.make_async_copy(
                ref.at[:, pl.ds(at, size)], held_ref.at[h, :, pl.ds(to, size)], in_sems.at[h, i]
            )
            for i, (ref, at, to, size) in enumerate(pieces)
        ]

    def store(h):
        return pltpu.make_async_copy(held_ref.at[h], out_ref.at[h], out_sems.at[h])

    for h in range(head_count):
        for fetch in fetches(h):
            fetch.start()
    for h in range(head_count):
        for fetch in fetches(h):
            fetch.wait()
        store(h).start()
    for h in range(head_count):
        store(h).wait()


def first_parts(key, value, query, head_count, width):
    shape = (head_count, query.shape[0], 2 * key.shape[1] // head_count + width)
    return pl.pallas_call(
        functools.partial(first_parts_kernel, head_count=head_count, width=width),
        in_specs=[pl.BlockSpec(memory_space=pl.ANY)] * 3,
        out_specs=pl.BlockSpec(memory_space=pl.ANY),
        out_shape=jax.ShapeDtypeStruct(shape, jnp.bfloat16),
        scratch_shapes=[
            pltpu.VMEM(shape, jnp.bfloat16),
            pltpu.SemaphoreType.DMA((head_count, 3)),
            pltpu.SemaphoreType.DMA((head_count,)),
        ],
        compiler_params=pltpu.CompilerParams(vmem_limit_bytes=VMEM_BYTES),
        name="first_parts",
    )(key, value, query)


def later_parts_kernel(place_ref, q_ref, *refs, chips, firsts, widths):
    chunks = len(widths)
    in_sems, out_sems = refs[-2:]
    held_refs, out_refs = refs[-2 - chunks : -2], refs[: -2 - chunks]
    core, chip = place_ref[0], place_ref[1]
    q_width = q_ref.shape[1] // (2 * chips)
    moves = []
    for chunk, (first, width) in enumerate(zip(firsts, widths)):
        outs = out_refs[chunk * (chips + 1) : (chunk + 1) * (chips + 1)]
        for side in range(2):
            for step in range(chips):
                member = lax.rem(chip + step, chips) * 2 + lax.rem(core + side, 2)
                column = pl.multiple_of(member * q_width + first, HD)
                held = held_refs[chunk].at[side * chips + step]
                at = (chunk * 2 + side) * chips + step
                out = outs[chips].at[step] if side else outs[step].at[0]
                moves.append((
                    pltpu.make_async_copy(q_ref.at[:, pl.ds(column, width)], held, in_sems.at[at]),
                    pltpu.make_async_copy(held, out, out_sems.at[at]),
                ))
    for fetch, _ in moves:
        fetch.start()
    for fetch, store in moves:
        fetch.wait()
        store.start()
    for _, store in moves:
        store.wait()


def later_parts(query, place, head_count, firsts, widths):
    rows, chips = query.shape[0], head_count // 2
    shapes = []
    for width in widths:
        shapes += [jax.ShapeDtypeStruct((2, rows, width), jnp.bfloat16)] * chips
        shapes.append(jax.ShapeDtypeStruct((chips, rows, width), jnp.bfloat16))
    copies = 2 * chips * len(widths)
    outs = pl.pallas_call(
        functools.partial(later_parts_kernel, chips=chips, firsts=firsts, widths=widths),
        in_specs=[pl.BlockSpec(memory_space=pltpu.SMEM), pl.BlockSpec(memory_space=pl.ANY)],
        out_specs=[pl.BlockSpec(memory_space=pl.ANY)] * len(shapes),
        out_shape=shapes,
        scratch_shapes=[pltpu.VMEM((2 * chips, rows, width), jnp.bfloat16) for width in widths]
        + [pltpu.SemaphoreType.DMA((copies,))] * 2,
        compiler_params=pltpu.CompilerParams(vmem_limit_bytes=VMEM_BYTES),
        cost_estimate=pl.CostEstimate(flops=0, bytes_accessed=4 * query.size, transcendentals=0),
        name="later_parts",
    )(place, query)
    split = [outs[(chips + 1) * i : (chips + 1) * (i + 1)] for i in range(len(widths))]
    return [list(part[:chips]) for part in split], [part[chips] for part in split]


def fill_kernel(got_ref, *refs):
    held_ref, in_sems, out_sems = refs[-3:]
    steps = held_ref.shape[0]
    out_refs = refs[steps : 2 * steps]
    fetches = [pltpu.make_async_copy(got_ref.at[i], held_ref.at[i], in_sems.at[i]) for i in range(steps)]
    stores = [pltpu.make_async_copy(held_ref.at[i], out_refs[i].at[1], out_sems.at[i]) for i in range(steps)]
    for fetch in fetches:
        fetch.start()
    for fetch, store in zip(fetches, stores):
        fetch.wait()
        store.start()
    for store in stores:
        store.wait()


def fill(parts, got):
    return pl.pallas_call(
        fill_kernel,
        in_specs=[pl.BlockSpec(memory_space=pl.ANY)] * (1 + len(parts)),
        out_specs=[pl.BlockSpec(memory_space=pl.ANY)] * len(parts),
        out_shape=[jax.ShapeDtypeStruct(part.shape, part.dtype) for part in parts],
        scratch_shapes=[pltpu.VMEM(got.shape, got.dtype)] + [pltpu.SemaphoreType.DMA((len(parts),))] * 2,
        input_output_aliases={1 + i: i for i in range(len(parts))},
        compiler_params=pltpu.CompilerParams(vmem_limit_bytes=VMEM_BYTES),
        cost_estimate=pl.CostEstimate(flops=0, bytes_accessed=0, transcendentals=0),
        name="fill",
    )(got, *parts)


def place_kernel(source_ref, *refs, count, first, width):
    received_ref, out_ref, held_ref, in_sems, out_sems = refs[0], refs[-4], refs[-3], refs[-2], refs[-1]

    def fetch(i):
        return pltpu.make_async_copy(received_ref.at[source_ref[i]], held_ref.at[i], in_sems.at[i])

    def store(i):
        return pltpu.make_async_copy(
            held_ref.at[i], out_ref.at[pl.ds(i * BLK, BLK), pl.ds(first, width)], out_sems.at[i]
        )

    for i in range(count):
        fetch(i).start()
    for i in range(count):
        fetch(i).wait()
        store(i).start()
    for i in range(count):
        store(i).wait()


def place(received, source, result, first, count, full_width):
    slots, _, width = received.shape
    given = [received] if result is None else [received, result]
    return pl.pallas_call(
        functools.partial(place_kernel, count=count, first=first, width=width),
        in_specs=[pl.BlockSpec(memory_space=pltpu.SMEM)] + [pl.BlockSpec(memory_space=pl.ANY)] * len(given),
        out_specs=pl.BlockSpec(memory_space=pl.ANY),
        out_shape=jax.ShapeDtypeStruct((count * BLK, full_width), jnp.bfloat16),
        scratch_shapes=[
            pltpu.VMEM((count, BLK, width), jnp.bfloat16),
            pltpu.SemaphoreType.DMA((count,)),
            pltpu.SemaphoreType.DMA((count,)),
        ],
        input_output_aliases={} if result is None else {2: 0},
        compiler_params=pltpu.CompilerParams(vmem_limit_bytes=SHARED_VMEM_BYTES),
        cost_estimate=pl.CostEstimate(flops=0, bytes_accessed=4 * count * BLK * width, transcendentals=0),
        name="place",
    )(source, *given)


def shards(query, key, value, doc_ids, plan):
    head_count = lax.axis_size("head")
    shard_count = lax.axis_size("ctx")
    local_rows = query.shape[0]
    rows = head_count * local_rows
    count = rows // BLK
    per_device = local_rows // BLK
    q_width = query.shape[1] // head_count
    shard = lax.axis_index("ctx").astype(jnp.int32)
    member = lax.axis_index("head").astype(jnp.int32)
    core, chip, chips = member % 2, member // 2, head_count // 2

    widths = [heads * HD for heads in CHUNKS]
    firsts = [sum(widths[:i]) for i in range(len(widths))]
    opening = first_parts(key, value, query, head_count, widths[0])
    kept, given = later_parts(query, jnp.stack([core, chip]), head_count, firsts[1:], widths[1:])
    swap = [(h, h ^ 1) for h in range(head_count)]
    later = [fill(parts, lax.ppermute(part, "head", swap)) for parts, part in zip(kept, given)]
    opening = lax.all_to_all(opening, "head", split_axis=0, concat_axis=0, tiled=True)

    index = jnp.arange(count, dtype=jnp.int32)
    own_ids = shard * count + index
    position = jnp.arange(plan.shape[0], dtype=jnp.int32)
    target = jnp.sum(
        jnp.where(plan[None, :] == own_ids[:, None], position[None, :] // count, 0), axis=1, dtype=jnp.int32
    )
    source = lax.dynamic_slice_in_dim(plan, shard * count, count) // count
    step_of, rest = index // (2 * per_device), index % (2 * per_device)
    giver = (chip - step_of + chips) % chips * 2 + (core + rest // per_device) % 2
    arrival = giver * per_device + rest % per_device

    opening, later, target, source, arrival = lax.optimization_barrier(
        (opening, later, target, source, arrival)
    )
    opening = opening.reshape(rows, 2 * HD + widths[0])
    halo = lax.ppermute(
        opening[rows - HALO * BLK :, : 2 * HD], "ctx", [(i, i + 1) for i in range(shard_count - 1)]
    )
    tables = (doc_ids, target, shard.reshape(1))

    result = None
    for turn, heads in enumerate(CHUNKS):
        if turn == 0:
            views = [(-1, None, i * BLK, 2 * HD) for i in range(count)]
            sent = attend(
                opening, None, [], views[MAXDOC:], index, heads, tables, count, shard_count, MAXDOC, count - MAXDOC
            )
            sent = attend(
                opening, halo, [], views[:MAXDOC], index, heads, tables, count, shard_count, 0, MAXDOC, sent
            )
        else:
            sources = []
            for step, part in enumerate(later[turn - 1]):
                onward = [(h, (h + 2 * step) % head_count) for h in range(head_count)]
                sources.append(lax.ppermute(part, "head", onward) if step else part)
            views = [
                (i // (2 * per_device), i // per_device % 2, i % per_device * BLK, 0) for i in range(count)
            ]
            sent = attend(opening, halo, sources, views, arrival, heads, tables, count, shard_count)
        received = lax.all_to_all(sent, "ctx", split_axis=0, concat_axis=0, tiled=True)
        result = place(received, source, result, firsts[turn], count, q_width)
    return result


def solution(mesh):
    return jax.shard_map(
        shards,
        mesh=mesh,
        in_specs=(
            P(("ctx", "head"), None),
            P(("ctx", "head"), None),
            P(("ctx", "head"), None),
            P(),
            P(),
        ),
        out_specs=P("ctx", "head"),
        check_vma=False,
    )
```

```python
import functools
import math

import jax
import jax.numpy as jnp
from jax import lax
from jax.experimental import pallas as pl
from jax.experimental.pallas import tpu as pltpu
from jax.sharding import PartitionSpec as P

HD = 128
BLK = 128
MAXDOC = 8
VMEM_BYTES = 60 * 1024 * 1024
SHARED_VMEM_BYTES = 32 * 1024 * 1024
HALO = MAXDOC - 1
CHUNKS = (2, 6)
EXP2_SCALE = math.log2(math.e) / math.sqrt(HD)


def attend_kernel(doc_ref, slot_ref, order_ref, shard_ref, *refs, heads, count, base, steps, ahead, paired, q_views):
    given, (out_ref, win_ref, held_ref, mixed_ref, kv_sems, q_sems, out_sems) = refs[:-7], refs[-7:]
    width = heads * HD
    own_ref = given[0]

    def copy_own():
        rows = (base + steps) * BLK
        return pltpu.make_async_copy(
            own_ref.at[pl.ds(0, rows), pl.ds(0, 2 * HD)], win_ref.at[pl.ds(ahead * BLK, rows)], kv_sems.at[0]
        )

    def copy_halo():
        return pltpu.make_async_copy(given[1], win_ref.at[pl.ds(0, ahead * BLK)], kv_sems.at[1])

    def copy_out(step):
        return pltpu.make_async_copy(
            mixed_ref.at[step], out_ref.at[slot_ref[base + step]], out_sems.at[step]
        )

    copy_own().start()
    if ahead:
        copy_halo().start()
    for view in range(steps):
        which, lead, row, column = q_views[view]
        source = given[which] if lead is None else given[which].at[lead]
        step = order_ref[view]
        pltpu.make_async_copy(
            source.at[pl.ds(row, BLK), pl.ds(column, width)], held_ref.at[step], q_sems.at[step]
        ).start()

    row = lax.broadcasted_iota(jnp.int32, (heads * BLK, BLK), 0) % BLK
    column = lax.broadcasted_iota(jnp.int32, (heads * BLK, BLK), 1)
    causal = column <= row
    copy_own().wait()
    if ahead:
        copy_halo().wait()

    lanes = 2 if paired else 1

    def per_turn(turn, _):
        at = lanes * turn
        first = base + at
        block = shard_ref[0] * count + first
        doc = doc_ref[block]
        tiles = jnp.int32(1)
        for back in range(1, MAXDOC):
            before = jnp.maximum(block - back, 0)
            tiles += jnp.where((block >= back) & (doc_ref[before] == doc), 1, 0)
        for lane in range(lanes):
            held = held_ref.at[at + lane]
            pltpu.make_async_copy(held, held, q_sems.at[at + lane]).wait()

        def with_tiles(tiles_of):
            windows = []
            for lane, n in enumerate(tiles_of):
                start = pl.multiple_of((first + lane + ahead + 1 - n) * BLK, BLK)
                windows.append(pl.ds(start, n * BLK))
            scores = []
            for lane, n in enumerate(tiles_of):
                queries = jnp.concatenate(
                    [held_ref[at + lane, :, head * HD : (head + 1) * HD] for head in range(heads)], axis=0
                )
                scores.append(lax.dot_general(
                    queries, win_ref[windows[lane], :HD], (((1,), (1,)), ((), ())),
                    preferred_element_type=jnp.float32,
                ))
            for lane, n in enumerate(tiles_of):
                last = jnp.where(causal, scores[lane][:, (n - 1) * BLK :], -jnp.inf)
                scores[lane] = (
                    last if n == 1 else jnp.concatenate([scores[lane][:, : (n - 1) * BLK], last], axis=1)
                )
            tops = [jnp.max(s, axis=1, keepdims=True) for s in scores]
            expos = [jnp.exp2((s - top) * EXP2_SCALE) for s, top in zip(scores, tops)]
            totals = [jnp.sum(e, axis=1, keepdims=True) for e in expos]
            sums = [
                jnp.dot(e.astype(jnp.bfloat16), win_ref[window, HD:], preferred_element_type=jnp.float32)
                for e, window in zip(expos, windows)
            ]
            for lane in range(len(tiles_of)):
                mixed = (sums[lane] / totals[lane]).astype(jnp.bfloat16)
                for head in range(heads):
                    mixed_ref[at + lane, :, head * HD : (head + 1) * HD] = mixed[head * BLK : (head + 1) * BLK]

        if paired:
            same = doc_ref[block + 1] == doc
            for n in range(1, MAXDOC + 1):
                if n < MAXDOC:
                    pl.when((tiles == n) & same)(functools.partial(with_tiles, (n, n + 1)))
                pl.when((tiles == n) & jnp.logical_not(same))(functools.partial(with_tiles, (n, 1)))
        else:
            for n in range(1, MAXDOC + 1):
                pl.when(tiles == n)(functools.partial(with_tiles, (n,)))
        for lane in range(lanes):
            copy_out(at + lane).start()
        return 0

    lax.fori_loop(0, steps // lanes, per_turn, 0)
    for step in range(steps):
        copy_out(step).wait()


def attend(own, halo, sources, q_views, order, heads, tables, count, slots, base=0, steps=None, result=None):
    doc_ids, slot, shard = tables
    steps = count if steps is None else steps
    width = heads * HD
    ahead = 0 if halo is None else HALO
    alone = steps < count
    given = [own] + ([] if halo is None else [halo])
    views = [(len(given) + which if which >= 0 else 0, lead, row, column) for which, lead, row, column in q_views]
    given = given + list(sources) + ([] if result is None else [result])
    smem, anywhere = pl.BlockSpec(memory_space=pltpu.SMEM), pl.BlockSpec(memory_space=pl.ANY)
    return pl.pallas_call(
        functools.partial(
            attend_kernel, heads=heads, count=count, base=base, steps=steps, ahead=ahead, paired=alone,
            q_views=views
        ),
        in_specs=[smem] * 4 + [anywhere] * len(given),
        out_specs=pl.BlockSpec(memory_space=pl.ANY),
        out_shape=jax.ShapeDtypeStruct((slots, BLK, width), jnp.bfloat16),
        scratch_shapes=[
            pltpu.VMEM(((base + steps + ahead) * BLK, 2 * HD), jnp.bfloat16),
            pltpu.VMEM((steps, BLK, width), jnp.bfloat16),
            pltpu.VMEM((steps, BLK, width), jnp.bfloat16),
            pltpu.SemaphoreType.DMA((2,)),
            pltpu.SemaphoreType.DMA((steps,)),
            pltpu.SemaphoreType.DMA((steps,)),
        ],
        input_output_aliases={} if result is None else {4 + len(given) - 1: 0},
        compiler_params=pltpu.CompilerParams(vmem_limit_bytes=VMEM_BYTES if alone else SHARED_VMEM_BYTES),
        cost_estimate=pl.CostEstimate(
            flops=10**12 if ahead else 0, bytes_accessed=0, transcendentals=0
        ),
        name="attend",
    )(doc_ids, slot, order, shard, *given)


def first_parts_kernel(k_ref, v_ref, q_ref, out_ref, held_ref, in_sems, out_sems, *, head_count, width):
    kv_width, q_width = k_ref.shape[1] // head_count, q_ref.shape[1] // head_count
    rows = q_ref.shape[0]

    def fetches(h):
        pieces = (
            (k_ref, h * kv_width, 0, kv_width),
            (v_ref, h * kv_width, kv_width, kv_width),
            (q_ref, h * q_width, 2 * kv_width, width),
        )
        return [
            pltpu.make_async_copy(
                ref.at[:, pl.ds(at, size)], held_ref.at[h, :, pl.ds(to, size)], in_sems.at[h, i]
            )
            for i, (ref, at, to, size) in enumerate(pieces)
        ]

    def store(h):
        return pltpu.make_async_copy(held_ref.at[h], out_ref.at[h], out_sems.at[h])

    for h in range(head_count):
        for fetch in fetches(h):
            fetch.start()
    for h in range(head_count):
        for fetch in fetches(h):
            fetch.wait()
        store(h).start()
    for h in range(head_count):
        store(h).wait()


def first_parts(key, value, query, head_count, width):
    shape = (head_count, query.shape[0], 2 * key.shape[1] // head_count + width)
    return pl.pallas_call(
        functools.partial(first_parts_kernel, head_count=head_count, width=width),
        in_specs=[pl.BlockSpec(memory_space=pl.ANY)] * 3,
        out_specs=pl.BlockSpec(memory_space=pl.ANY),
        out_shape=jax.ShapeDtypeStruct(shape, jnp.bfloat16),
        scratch_shapes=[
            pltpu.VMEM(shape, jnp.bfloat16),
            pltpu.SemaphoreType.DMA((head_count, 3)),
            pltpu.SemaphoreType.DMA((head_count,)),
        ],
        compiler_params=pltpu.CompilerParams(vmem_limit_bytes=VMEM_BYTES),
        name="first_parts",
    )(key, value, query)


def later_parts_kernel(place_ref, q_ref, *refs, chips, firsts, widths):
    chunks = len(widths)
    in_sems, out_sems = refs[-2:]
    held_refs, out_refs = refs[-2 - chunks : -2], refs[: -2 - chunks]
    core, chip = place_ref[0], place_ref[1]
    q_width = q_ref.shape[1] // (2 * chips)
    moves = []
    for chunk, (first, width) in enumerate(zip(firsts, widths)):
        outs = out_refs[chunk * (chips + 1) : (chunk + 1) * (chips + 1)]
        for side in range(2):
            for step in range(chips):
                member = lax.rem(chip + step, chips) * 2 + lax.rem(core + side, 2)
                column = pl.multiple_of(member * q_width + first, HD)
                held = held_refs[chunk].at[side * chips + step]
                at = (chunk * 2 + side) * chips + step
                out = outs[chips].at[step] if side else outs[step].at[0]
                moves.append((
                    pltpu.make_async_copy(q_ref.at[:, pl.ds(column, width)], held, in_sems.at[at]),
                    pltpu.make_async_copy(held, out, out_sems.at[at]),
                ))
    for fetch, _ in moves:
        fetch.start()
    for fetch, store in moves:
        fetch.wait()
        store.start()
    for _, store in moves:
        store.wait()


def later_parts(query, place, head_count, firsts, widths):
    rows, chips = query.shape[0], head_count // 2
    shapes = []
    for width in widths:
        shapes += [jax.ShapeDtypeStruct((2, rows, width), jnp.bfloat16)] * chips
        shapes.append(jax.ShapeDtypeStruct((chips, rows, width), jnp.bfloat16))
    copies = 2 * chips * len(widths)
    outs = pl.pallas_call(
        functools.partial(later_parts_kernel, chips=chips, firsts=firsts, widths=widths),
        in_specs=[pl.BlockSpec(memory_space=pltpu.SMEM), pl.BlockSpec(memory_space=pl.ANY)],
        out_specs=[pl.BlockSpec(memory_space=pl.ANY)] * len(shapes),
        out_shape=shapes,
        scratch_shapes=[pltpu.VMEM((2 * chips, rows, width), jnp.bfloat16) for width in widths]
        + [pltpu.SemaphoreType.DMA((copies,))] * 2,
        compiler_params=pltpu.CompilerParams(vmem_limit_bytes=VMEM_BYTES),
        cost_estimate=pl.CostEstimate(flops=0, bytes_accessed=4 * query.size, transcendentals=0),
        name="later_parts",
    )(place, query)
    split = [outs[(chips + 1) * i : (chips + 1) * (i + 1)] for i in range(len(widths))]
    return [list(part[:chips]) for part in split], [part[chips] for part in split]


def fill_kernel(got_ref, *refs):
    held_ref, in_sems, out_sems = refs[-3:]
    steps = held_ref.shape[0]
    out_refs = refs[steps : 2 * steps]
    fetches = [pltpu.make_async_copy(got_ref.at[i], held_ref.at[i], in_sems.at[i]) for i in range(steps)]
    stores = [pltpu.make_async_copy(held_ref.at[i], out_refs[i].at[1], out_sems.at[i]) for i in range(steps)]
    for fetch in fetches:
        fetch.start()
    for fetch, store in zip(fetches, stores):
        fetch.wait()
        store.start()
    for store in stores:
        store.wait()


def fill(parts, got):
    return pl.pallas_call(
        fill_kernel,
        in_specs=[pl.BlockSpec(memory_space=pl.ANY)] * (1 + len(parts)),
        out_specs=[pl.BlockSpec(memory_space=pl.ANY)] * len(parts),
        out_shape=[jax.ShapeDtypeStruct(part.shape, part.dtype) for part in parts],
        scratch_shapes=[pltpu.VMEM(got.shape, got.dtype)] + [pltpu.SemaphoreType.DMA((len(parts),))] * 2,
        input_output_aliases={1 + i: i for i in range(len(parts))},
        compiler_params=pltpu.CompilerParams(vmem_limit_bytes=VMEM_BYTES),
        cost_estimate=pl.CostEstimate(flops=0, bytes_accessed=0, transcendentals=0),
        name="fill",
    )(got, *parts)


def place_kernel(source_ref, *refs, count, first, width):
    received_ref, out_ref, held_ref, in_sems, out_sems = refs[0], refs[-4], refs[-3], refs[-2], refs[-1]

    def fetch(i):
        return pltpu.make_async_copy(received_ref.at[source_ref[i]], held_ref.at[i], in_sems.at[i])

    def store(i):
        return pltpu.make_async_copy(
            held_ref.at[i], out_ref.at[pl.ds(i * BLK, BLK), pl.ds(first, width)], out_sems.at[i]
        )

    for i in range(count):
        fetch(i).start()
    for i in range(count):
        fetch(i).wait()
        store(i).start()
    for i in range(count):
        store(i).wait()


def place(received, source, result, first, count, full_width):
    slots, _, width = received.shape
    given = [received] if result is None else [received, result]
    return pl.pallas_call(
        functools.partial(place_kernel, count=count, first=first, width=width),
        in_specs=[pl.BlockSpec(memory_space=pltpu.SMEM)] + [pl.BlockSpec(memory_space=pl.ANY)] * len(given),
        out_specs=pl.BlockSpec(memory_space=pl.ANY),
        out_shape=jax.ShapeDtypeStruct((count * BLK, full_width), jnp.bfloat16),
        scratch_shapes=[
            pltpu.VMEM((count, BLK, width), jnp.bfloat16),
            pltpu.SemaphoreType.DMA((count,)),
            pltpu.SemaphoreType.DMA((count,)),
        ],
        input_output_aliases={} if result is None else {2: 0},
        compiler_params=pltpu.CompilerParams(vmem_limit_bytes=SHARED_VMEM_BYTES),
        cost_estimate=pl.CostEstimate(flops=0, bytes_accessed=4 * count * BLK * width, transcendentals=0),
        name="place",
    )(source, *given)


def shards(query, key, value, doc_ids, plan):
    head_count = lax.axis_size("head")
    shard_count = lax.axis_size("ctx")
    local_rows = query.shape[0]
    rows = head_count * local_rows
    count = rows // BLK
    per_device = local_rows // BLK
    q_width = query.shape[1] // head_count
    shard = lax.axis_index("ctx").astype(jnp.int32)
    member = lax.axis_index("head").astype(jnp.int32)
    core, chip, chips = member % 2, member // 2, head_count // 2

    widths = [heads * HD for heads in CHUNKS]
    firsts = [sum(widths[:i]) for i in range(len(widths))]
    opening = first_parts(key, value, query, head_count, widths[0])
    kept, given = later_parts(query, jnp.stack([core, chip]), head_count, firsts[1:], widths[1:])
    swap = [(h, h ^ 1) for h in range(head_count)]
    later = [fill(parts, lax.ppermute(part, "head", swap)) for parts, part in zip(kept, given)]
    opening = lax.all_to_all(opening, "head", split_axis=0, concat_axis=0, tiled=True)

    index = jnp.arange(count, dtype=jnp.int32)
    own_ids = shard * count + index
    position = jnp.arange(plan.shape[0], dtype=jnp.int32)
    target = jnp.sum(
        jnp.where(plan[None, :] == own_ids[:, None], position[None, :] // count, 0), axis=1, dtype=jnp.int32
    )
    source = lax.dynamic_slice_in_dim(plan, shard * count, count) // count
    step_of, rest = index // (2 * per_device), index % (2 * per_device)
    giver = (chip - step_of + chips) % chips * 2 + (core + rest // per_device) % 2
    arrival = giver * per_device + rest % per_device

    opening, later, target, source, arrival = lax.optimization_barrier(
        (opening, later, target, source, arrival)
    )
    opening = opening.reshape(rows, 2 * HD + widths[0])
    halo = lax.ppermute(
        opening[rows - HALO * BLK :, : 2 * HD], "ctx", [(i, i + 1) for i in range(shard_count - 1)]
    )
    tables = (doc_ids, target, shard.reshape(1))

    result = None
    for turn, heads in enumerate(CHUNKS):
        if turn == 0:
            views = [(-1, None, i * BLK, 2 * HD) for i in range(count)]
            sent = attend(
                opening, None, [], views[MAXDOC:], index, heads, tables, count, shard_count, MAXDOC, count - MAXDOC
            )
            sent = attend(
                opening, halo, [], views[:MAXDOC], index, heads, tables, count, shard_count, 0, MAXDOC, sent
            )
        else:
            sources = []
            for step, part in enumerate(later[turn - 1]):
                onward = [(h, (h + 2 * step) % head_count) for h in range(head_count)]
                sources.append(lax.ppermute(part, "head", onward) if step else part)
            views = [
                (i // (2 * per_device), i // per_device % 2, i % per_device * BLK, 0) for i in range(count)
            ]
            sent = attend(opening, halo, sources, views, arrival, heads, tables, count, shard_count)
        received = lax.all_to_all(sent, "ctx", split_axis=0, concat_axis=0, tiled=True)
        result = place(received, source, result, firsts[turn], count, q_width)
    return result


def solution(mesh):
    return jax.shard_map(
        shards,
        mesh=mesh,
        in_specs=(
            P(("ctx", "head"), None),
            P(("ctx", "head"), None),
            P(("ctx", "head"), None),
            P(),
            P(),
        ),
        out_specs=P("ctx", "head"),
        check_vma=False,
    )
```

```python
import functools
import math

import jax
import jax.numpy as jnp
from jax import lax
from jax.experimental import pallas as pl
from jax.experimental.pallas import tpu as pltpu
from jax.sharding import PartitionSpec as P

HD = 128
BLK = 128
MAXDOC = 8
VMEM_BYTES = 60 * 1024 * 1024
SHARED_VMEM_BYTES = 32 * 1024 * 1024
HALO = MAXDOC - 1
CHUNKS = (2, 6)
EXP2_SCALE = math.log2(math.e) / math.sqrt(HD)


def attend_kernel(doc_ref, slot_ref, shard_ref, *refs, heads, count, base, steps, ahead, paired, ordered, q_views):
    order_ref, refs = (refs[0], refs[1:]) if ordered else (None, refs)
    given, (out_ref, win_ref, held_ref, mixed_ref, kv_sems, q_sems, out_sems) = refs[:-7], refs[-7:]
    width = heads * HD
    own_ref = given[0]

    def copy_own():
        rows = (base + steps) * BLK
        return pltpu.make_async_copy(
            own_ref.at[pl.ds(0, rows), pl.ds(0, 2 * HD)], win_ref.at[pl.ds(ahead * BLK, rows)], kv_sems.at[0]
        )

    def copy_halo():
        return pltpu.make_async_copy(given[1], win_ref.at[pl.ds(0, ahead * BLK)], kv_sems.at[1])

    def copy_out(step):
        return pltpu.make_async_copy(
            mixed_ref.at[step], out_ref.at[slot_ref[base + step]], out_sems.at[step]
        )

    copy_own().start()
    if ahead:
        copy_halo().start()
    for view in range(steps):
        which, lead, row, column = q_views[view]
        source = given[which] if lead is None else given[which].at[lead]
        step = order_ref[view] if ordered else view
        pltpu.make_async_copy(
            source.at[pl.ds(row, BLK), pl.ds(column, width)], held_ref.at[step], q_sems.at[step]
        ).start()

    row = lax.broadcasted_iota(jnp.int32, (heads * BLK, BLK), 0) % BLK
    column = lax.broadcasted_iota(jnp.int32, (heads * BLK, BLK), 1)
    causal = column <= row
    copy_own().wait()
    if ahead:
        copy_halo().wait()

    lanes = 2 if paired else 1

    def per_turn(turn, _):
        at = lanes * turn
        first = base + at
        block = shard_ref[0] * count + first
        doc = doc_ref[block]
        tiles = jnp.int32(1)
        for back in range(1, MAXDOC):
            before = jnp.maximum(block - back, 0)
            tiles += jnp.where((block >= back) & (doc_ref[before] == doc), 1, 0)
        for lane in range(lanes):
            held = held_ref.at[at + lane]
            pltpu.make_async_copy(held, held, q_sems.at[at + lane]).wait()

        def with_tiles(tiles_of):
            windows = []
            for lane, n in enumerate(tiles_of):
                start = pl.multiple_of((first + lane + ahead + 1 - n) * BLK, BLK)
                windows.append(pl.ds(start, n * BLK))
            scores = []
            for lane, n in enumerate(tiles_of):
                queries = jnp.concatenate(
                    [held_ref[at + lane, :, head * HD : (head + 1) * HD] for head in range(heads)], axis=0
                )
                scores.append(lax.dot_general(
                    queries, win_ref[windows[lane], :HD], (((1,), (1,)), ((), ())),
                    preferred_element_type=jnp.float32,
                ))
            for lane, n in enumerate(tiles_of):
                last = jnp.where(causal, scores[lane][:, (n - 1) * BLK :], -jnp.inf)
                scores[lane] = (
                    last if n == 1 else jnp.concatenate([scores[lane][:, : (n - 1) * BLK], last], axis=1)
                )
            tops = [jnp.max(s, axis=1, keepdims=True) for s in scores]
            expos = [jnp.exp2((s - top) * EXP2_SCALE) for s, top in zip(scores, tops)]
            totals = [jnp.sum(e, axis=1, keepdims=True) for e in expos]
            sums = [
                jnp.dot(e.astype(jnp.bfloat16), win_ref[window, HD:], preferred_element_type=jnp.float32)
                for e, window in zip(expos, windows)
            ]
            for lane in range(len(tiles_of)):
                mixed = (sums[lane] / totals[lane]).astype(jnp.bfloat16)
                for head in range(heads):
                    mixed_ref[at + lane, :, head * HD : (head + 1) * HD] = mixed[head * BLK : (head + 1) * BLK]

        if paired:
            same = doc_ref[block + 1] == doc
            for n in range(1, MAXDOC + 1):
                if n < MAXDOC:
                    pl.when((tiles == n) & same)(functools.partial(with_tiles, (n, n + 1)))
                pl.when((tiles == n) & jnp.logical_not(same))(functools.partial(with_tiles, (n, 1)))
        else:
            for n in range(1, MAXDOC + 1):
                pl.when(tiles == n)(functools.partial(with_tiles, (n,)))
        for lane in range(lanes):
            copy_out(at + lane).start()
        return 0

    lax.fori_loop(0, steps // lanes, per_turn, 0)
    for step in range(steps):
        copy_out(step).wait()


def attend(own, halo, sources, q_views, order, heads, tables, count, slots, base=0, steps=None, result=None):
    doc_ids, slot, shard = tables
    steps = count if steps is None else steps
    width = heads * HD
    ahead = 0 if halo is None else HALO
    alone = steps < count
    given = [own] + ([] if halo is None else [halo])
    views = [(len(given) + which if which >= 0 else 0, lead, row, column) for which, lead, row, column in q_views]
    given = given + list(sources) + ([] if result is None else [result])
    scalars = [doc_ids, slot, shard] + ([] if order is None else [order])
    smem, anywhere = pl.BlockSpec(memory_space=pltpu.SMEM), pl.BlockSpec(memory_space=pl.ANY)
    return pl.pallas_call(
        functools.partial(
            attend_kernel, heads=heads, count=count, base=base, steps=steps, ahead=ahead, paired=alone,
            ordered=order is not None, q_views=views
        ),
        in_specs=[smem] * len(scalars) + [anywhere] * len(given),
        out_specs=pl.BlockSpec(memory_space=pl.ANY),
        out_shape=jax.ShapeDtypeStruct((slots, BLK, width), jnp.bfloat16),
        scratch_shapes=[
            pltpu.VMEM(((base + steps + ahead) * BLK, 2 * HD), jnp.bfloat16),
            pltpu.VMEM((steps, BLK, width), jnp.bfloat16),
            pltpu.VMEM((steps, BLK, width), jnp.bfloat16),
            pltpu.SemaphoreType.DMA((2,)),
            pltpu.SemaphoreType.DMA((steps,)),
            pltpu.SemaphoreType.DMA((steps,)),
        ],
        input_output_aliases={} if result is None else {len(scalars) + len(given) - 1: 0},
        compiler_params=pltpu.CompilerParams(vmem_limit_bytes=VMEM_BYTES if alone else SHARED_VMEM_BYTES),
        cost_estimate=pl.CostEstimate(
            flops=10**12 if ahead else 0, bytes_accessed=0, transcendentals=0
        ),
        name="attend",
    )(*scalars, *given)


def first_parts_kernel(k_ref, v_ref, q_ref, out_ref, held_ref, in_sems, out_sems, *, head_count, width):
    kv_width, q_width = k_ref.shape[1] // head_count, q_ref.shape[1] // head_count
    rows = q_ref.shape[0]

    def fetches(h):
        pieces = (
            (k_ref, h * kv_width, 0, kv_width),
            (v_ref, h * kv_width, kv_width, kv_width),
            (q_ref, h * q_width, 2 * kv_width, width),
        )
        return [
            pltpu.make_async_copy(
                ref.at[:, pl.ds(at, size)], held_ref.at[h, :, pl.ds(to, size)], in_sems.at[h, i]
            )
            for i, (ref, at, to, size) in enumerate(pieces)
        ]

    def store(h):
        return pltpu.make_async_copy(held_ref.at[h], out_ref.at[h], out_sems.at[h])

    for h in range(head_count):
        for fetch in fetches(h):
            fetch.start()
    for h in range(head_count):
        for fetch in fetches(h):
            fetch.wait()
        store(h).start()
    for h in range(head_count):
        store(h).wait()


def first_parts(key, value, query, head_count, width):
    shape = (head_count, query.shape[0], 2 * key.shape[1] // head_count + width)
    return pl.pallas_call(
        functools.partial(first_parts_kernel, head_count=head_count, width=width),
        in_specs=[pl.BlockSpec(memory_space=pl.ANY)] * 3,
        out_specs=pl.BlockSpec(memory_space=pl.ANY),
        out_shape=jax.ShapeDtypeStruct(shape, jnp.bfloat16),
        scratch_shapes=[
            pltpu.VMEM(shape, jnp.bfloat16),
            pltpu.SemaphoreType.DMA((head_count, 3)),
            pltpu.SemaphoreType.DMA((head_count,)),
        ],
        compiler_params=pltpu.CompilerParams(vmem_limit_bytes=VMEM_BYTES),
        name="first_parts",
    )(key, value, query)


def later_parts_kernel(place_ref, q_ref, *refs, chips, firsts, widths):
    chunks = len(widths)
    in_sems, out_sems = refs[-2:]
    held_refs, out_refs = refs[-2 - chunks : -2], refs[: -2 - chunks]
    core, chip = place_ref[0], place_ref[1]
    q_width = q_ref.shape[1] // (2 * chips)
    moves = []
    for chunk, (first, width) in enumerate(zip(firsts, widths)):
        outs = out_refs[chunk * (chips + 1) : (chunk + 1) * (chips + 1)]
        for side in range(2):
            for step in range(chips):
                member = lax.rem(chip + step, chips) * 2 + lax.rem(core + side, 2)
                column = pl.multiple_of(member * q_width + first, HD)
                held = held_refs[chunk].at[side * chips + step]
                at = (chunk * 2 + side) * chips + step
                out = outs[chips].at[step] if side else outs[step].at[0]
                moves.append((
                    pltpu.make_async_copy(q_ref.at[:, pl.ds(column, width)], held, in_sems.at[at]),
                    pltpu.make_async_copy(held, out, out_sems.at[at]),
                ))
    for fetch, _ in moves:
        fetch.start()
    for fetch, store in moves:
        fetch.wait()
        store.start()
    for _, store in moves:
        store.wait()


def later_parts(query, place, head_count, firsts, widths):
    rows, chips = query.shape[0], head_count // 2
    shapes = []
    for width in widths:
        shapes += [jax.ShapeDtypeStruct((2, rows, width), jnp.bfloat16)] * chips
        shapes.append(jax.ShapeDtypeStruct((chips, rows, width), jnp.bfloat16))
    copies = 2 * chips * len(widths)
    outs = pl.pallas_call(
        functools.partial(later_parts_kernel, chips=chips, firsts=firsts, widths=widths),
        in_specs=[pl.BlockSpec(memory_space=pltpu.SMEM), pl.BlockSpec(memory_space=pl.ANY)],
        out_specs=[pl.BlockSpec(memory_space=pl.ANY)] * len(shapes),
        out_shape=shapes,
        scratch_shapes=[pltpu.VMEM((2 * chips, rows, width), jnp.bfloat16) for width in widths]
        + [pltpu.SemaphoreType.DMA((copies,))] * 2,
        compiler_params=pltpu.CompilerParams(vmem_limit_bytes=VMEM_BYTES),
        cost_estimate=pl.CostEstimate(flops=0, bytes_accessed=4 * query.size, transcendentals=0),
        name="later_parts",
    )(place, query)
    split = [outs[(chips + 1) * i : (chips + 1) * (i + 1)] for i in range(len(widths))]
    return [list(part[:chips]) for part in split], [part[chips] for part in split]


def fill_kernel(got_ref, *refs):
    held_ref, in_sems, out_sems = refs[-3:]
    steps = held_ref.shape[0]
    out_refs = refs[steps : 2 * steps]
    fetches = [pltpu.make_async_copy(got_ref.at[i], held_ref.at[i], in_sems.at[i]) for i in range(steps)]
    stores = [pltpu.make_async_copy(held_ref.at[i], out_refs[i].at[1], out_sems.at[i]) for i in range(steps)]
    for fetch in fetches:
        fetch.start()
    for fetch, store in zip(fetches, stores):
        fetch.wait()
        store.start()
    for store in stores:
        store.wait()


def fill(parts, got):
    return pl.pallas_call(
        fill_kernel,
        in_specs=[pl.BlockSpec(memory_space=pl.ANY)] * (1 + len(parts)),
        out_specs=[pl.BlockSpec(memory_space=pl.ANY)] * len(parts),
        out_shape=[jax.ShapeDtypeStruct(part.shape, part.dtype) for part in parts],
        scratch_shapes=[pltpu.VMEM(got.shape, got.dtype)] + [pltpu.SemaphoreType.DMA((len(parts),))] * 2,
        input_output_aliases={1 + i: i for i in range(len(parts))},
        compiler_params=pltpu.CompilerParams(vmem_limit_bytes=VMEM_BYTES),
        cost_estimate=pl.CostEstimate(flops=0, bytes_accessed=0, transcendentals=0),
        name="fill",
    )(got, *parts)


def place_kernel(source_ref, *refs, count, first, width):
    received_ref, out_ref, held_ref, in_sems, out_sems = refs[0], refs[-4], refs[-3], refs[-2], refs[-1]

    def fetch(i):
        return pltpu.make_async_copy(received_ref.at[source_ref[i]], held_ref.at[i], in_sems.at[i])

    def store(i):
        return pltpu.make_async_copy(
            held_ref.at[i], out_ref.at[pl.ds(i * BLK, BLK), pl.ds(first, width)], out_sems.at[i]
        )

    for i in range(count):
        fetch(i).start()
    for i in range(count):
        fetch(i).wait()
        store(i).start()
    for i in range(count):
        store(i).wait()


def place(received, source, result, first, count, full_width):
    slots, _, width = received.shape
    given = [received] if result is None else [received, result]
    return pl.pallas_call(
        functools.partial(place_kernel, count=count, first=first, width=width),
        in_specs=[pl.BlockSpec(memory_space=pltpu.SMEM)] + [pl.BlockSpec(memory_space=pl.ANY)] * len(given),
        out_specs=pl.BlockSpec(memory_space=pl.ANY),
        out_shape=jax.ShapeDtypeStruct((count * BLK, full_width), jnp.bfloat16),
        scratch_shapes=[
            pltpu.VMEM((count, BLK, width), jnp.bfloat16),
            pltpu.SemaphoreType.DMA((count,)),
            pltpu.SemaphoreType.DMA((count,)),
        ],
        input_output_aliases={} if result is None else {2: 0},
        compiler_params=pltpu.CompilerParams(vmem_limit_bytes=SHARED_VMEM_BYTES),
        cost_estimate=pl.CostEstimate(flops=0, bytes_accessed=4 * count * BLK * width, transcendentals=0),
        name="place",
    )(source, *given)


def shards(query, key, value, doc_ids, plan):
    head_count = lax.axis_size("head")
    shard_count = lax.axis_size("ctx")
    local_rows = query.shape[0]
    rows = head_count * local_rows
    count = rows // BLK
    per_device = local_rows // BLK
    q_width = query.shape[1] // head_count
    shard = lax.axis_index("ctx").astype(jnp.int32)
    member = lax.axis_index("head").astype(jnp.int32)
    core, chip, chips = member % 2, member // 2, head_count // 2

    widths = [heads * HD for heads in CHUNKS]
    firsts = [sum(widths[:i]) for i in range(len(widths))]
    opening = first_parts(key, value, query, head_count, widths[0])
    kept, given = later_parts(query, jnp.stack([core, chip]), head_count, firsts[1:], widths[1:])
    swap = [(h, h ^ 1) for h in range(head_count)]
    later = [fill(parts, lax.ppermute(part, "head", swap)) for parts, part in zip(kept, given)]
    opening = lax.all_to_all(opening, "head", split_axis=0, concat_axis=0, tiled=True)

    index = jnp.arange(count, dtype=jnp.int32)
    own_ids = shard * count + index
    position = jnp.arange(plan.shape[0], dtype=jnp.int32)
    target = jnp.sum(
        jnp.where(plan[None, :] == own_ids[:, None], position[None, :] // count, 0), axis=1, dtype=jnp.int32
    )
    source = lax.dynamic_slice_in_dim(plan, shard * count, count) // count
    step_of, rest = index // (2 * per_device), index % (2 * per_device)
    giver = (chip - step_of + chips) % chips * 2 + (core + rest // per_device) % 2
    arrival = giver * per_device + rest % per_device

    opening, later, target, source, arrival = lax.optimization_barrier(
        (opening, later, target, source, arrival)
    )
    opening = opening.reshape(rows, 2 * HD + widths[0])
    halo = lax.ppermute(
        opening[rows - HALO * BLK :, : 2 * HD], "ctx", [(i, i + 1) for i in range(shard_count - 1)]
    )
    tables = (doc_ids, target, shard.reshape(1))

    result = None
    for turn, heads in enumerate(CHUNKS):
        if turn == 0:
            views = [(-1, None, i * BLK, 2 * HD) for i in range(count)]
            sent = attend(
                opening, None, [], views[MAXDOC:], None, heads, tables, count, shard_count, MAXDOC, count - MAXDOC
            )
            sent = attend(
                opening, halo, [], views[:MAXDOC], None, heads, tables, count, shard_count, 0, MAXDOC, sent
            )
        else:
            sources = []
            for step, part in enumerate(later[turn - 1]):
                onward = [(h, (h + 2 * step) % head_count) for h in range(head_count)]
                sources.append(lax.ppermute(part, "head", onward) if step else part)
            views = [
                (i // (2 * per_device), i // per_device % 2, i % per_device * BLK, 0) for i in range(count)
            ]
            sent = attend(opening, halo, sources, views, arrival, heads, tables, count, shard_count)
        received = lax.all_to_all(sent, "ctx", split_axis=0, concat_axis=0, tiled=True)
        result = place(received, source, result, firsts[turn], count, q_width)
    return result


def solution(mesh):
    return jax.shard_map(
        shards,
        mesh=mesh,
        in_specs=(
            P(("ctx", "head"), None),
            P(("ctx", "head"), None),
            P(("ctx", "head"), None),
            P(),
            P(),
        ),
        out_specs=P("ctx", "head"),
        check_vma=False,
    )
```

```python
import functools
import math

import jax
import jax.numpy as jnp
from jax import lax
from jax.experimental import pallas as pl
from jax.experimental.pallas import tpu as pltpu
from jax.sharding import PartitionSpec as P

HD = 128
BLK = 128
MAXDOC = 8
VMEM_BYTES = 60 * 1024 * 1024
SHARED_VMEM_BYTES = 32 * 1024 * 1024
HALO = MAXDOC - 1
CHUNKS = (1, 3, 4)
EXP2_SCALE = math.log2(math.e) / math.sqrt(HD)


def attend_kernel(doc_ref, slot_ref, shard_ref, *refs, heads, count, base, steps, ahead, paired, ordered, q_views):
    order_ref, refs = (refs[0], refs[1:]) if ordered else (None, refs)
    given, (out_ref, win_ref, held_ref, mixed_ref, kv_sems, q_sems, out_sems) = refs[:-7], refs[-7:]
    width = heads * HD
    own_ref = given[0]

    def copy_own():
        rows = (base + steps) * BLK
        return pltpu.make_async_copy(
            own_ref.at[pl.ds(0, rows), pl.ds(0, 2 * HD)], win_ref.at[pl.ds(ahead * BLK, rows)], kv_sems.at[0]
        )

    def copy_halo():
        return pltpu.make_async_copy(given[1], win_ref.at[pl.ds(0, ahead * BLK)], kv_sems.at[1])

    def copy_out(step):
        return pltpu.make_async_copy(
            mixed_ref.at[step], out_ref.at[slot_ref[base + step]], out_sems.at[step]
        )

    copy_own().start()
    if ahead:
        copy_halo().start()
    for view in range(steps):
        which, lead, row, column = q_views[view]
        source = given[which] if lead is None else given[which].at[lead]
        step = order_ref[view] if ordered else view
        pltpu.make_async_copy(
            source.at[pl.ds(row, BLK), pl.ds(column, width)], held_ref.at[step], q_sems.at[step]
        ).start()

    row = lax.broadcasted_iota(jnp.int32, (heads * BLK, BLK), 0) % BLK
    column = lax.broadcasted_iota(jnp.int32, (heads * BLK, BLK), 1)
    causal = column <= row
    copy_own().wait()
    if ahead:
        copy_halo().wait()

    lanes = 2 if paired else 1

    def per_turn(turn, _):
        at = lanes * turn
        first = base + at
        block = shard_ref[0] * count + first
        doc = doc_ref[block]
        tiles = jnp.int32(1)
        for back in range(1, MAXDOC):
            before = jnp.maximum(block - back, 0)
            tiles += jnp.where((block >= back) & (doc_ref[before] == doc), 1, 0)
        for lane in range(lanes):
            held = held_ref.at[at + lane]
            pltpu.make_async_copy(held, held, q_sems.at[at + lane]).wait()

        def with_tiles(tiles_of):
            windows = []
            for lane, n in enumerate(tiles_of):
                start = pl.multiple_of((first + lane + ahead + 1 - n) * BLK, BLK)
                windows.append(pl.ds(start, n * BLK))
            scores = []
            for lane, n in enumerate(tiles_of):
                queries = jnp.concatenate(
                    [held_ref[at + lane, :, head * HD : (head + 1) * HD] for head in range(heads)], axis=0
                )
                scores.append(lax.dot_general(
                    queries, win_ref[windows[lane], :HD], (((1,), (1,)), ((), ())),
                    preferred_element_type=jnp.float32,
                ))
            for lane, n in enumerate(tiles_of):
                last = jnp.where(causal, scores[lane][:, (n - 1) * BLK :], -jnp.inf)
                scores[lane] = (
                    last if n == 1 else jnp.concatenate([scores[lane][:, : (n - 1) * BLK], last], axis=1)
                )
            tops = [jnp.max(s, axis=1, keepdims=True) for s in scores]
            expos = [jnp.exp2((s - top) * EXP2_SCALE) for s, top in zip(scores, tops)]
            totals = [jnp.sum(e, axis=1, keepdims=True) for e in expos]
            sums = [
                jnp.dot(e.astype(jnp.bfloat16), win_ref[window, HD:], preferred_element_type=jnp.float32)
                for e, window in zip(expos, windows)
            ]
            for lane in range(len(tiles_of)):
                mixed = (sums[lane] / totals[lane]).astype(jnp.bfloat16)
                for head in range(heads):
                    mixed_ref[at + lane, :, head * HD : (head + 1) * HD] = mixed[head * BLK : (head + 1) * BLK]

        if paired:
            same = doc_ref[block + 1] == doc
            for n in range(1, MAXDOC + 1):
                if n < MAXDOC:
                    pl.when((tiles == n) & same)(functools.partial(with_tiles, (n, n + 1)))
                pl.when((tiles == n) & jnp.logical_not(same))(functools.partial(with_tiles, (n, 1)))
        else:
            for n in range(1, MAXDOC + 1):
                pl.when(tiles == n)(functools.partial(with_tiles, (n,)))
        for lane in range(lanes):
            copy_out(at + lane).start()
        return 0

    lax.fori_loop(0, steps // lanes, per_turn, 0)
    for step in range(steps):
        copy_out(step).wait()


def attend(own, halo, sources, q_views, order, heads, tables, count, slots, base=0, steps=None, result=None):
    doc_ids, slot, shard = tables
    steps = count if steps is None else steps
    width = heads * HD
    ahead = 0 if halo is None else HALO
    alone = steps < count
    given = [own] + ([] if halo is None else [halo])
    views = [(len(given) + which if which >= 0 else 0, lead, row, column) for which, lead, row, column in q_views]
    given = given + list(sources) + ([] if result is None else [result])
    scalars = [doc_ids, slot, shard] + ([] if order is None else [order])
    smem, anywhere = pl.BlockSpec(memory_space=pltpu.SMEM), pl.BlockSpec(memory_space=pl.ANY)
    return pl.pallas_call(
        functools.partial(
            attend_kernel, heads=heads, count=count, base=base, steps=steps, ahead=ahead, paired=alone,
            ordered=order is not None, q_views=views
        ),
        in_specs=[smem] * len(scalars) + [anywhere] * len(given),
        out_specs=pl.BlockSpec(memory_space=pl.ANY),
        out_shape=jax.ShapeDtypeStruct((slots, BLK, width), jnp.bfloat16),
        scratch_shapes=[
            pltpu.VMEM(((base + steps + ahead) * BLK, 2 * HD), jnp.bfloat16),
            pltpu.VMEM((steps, BLK, width), jnp.bfloat16),
            pltpu.VMEM((steps, BLK, width), jnp.bfloat16),
            pltpu.SemaphoreType.DMA((2,)),
            pltpu.SemaphoreType.DMA((steps,)),
            pltpu.SemaphoreType.DMA((steps,)),
        ],
        input_output_aliases={} if result is None else {len(scalars) + len(given) - 1: 0},
        compiler_params=pltpu.CompilerParams(vmem_limit_bytes=VMEM_BYTES if alone else SHARED_VMEM_BYTES),
        cost_estimate=pl.CostEstimate(
            flops=10**12 if ahead else 0, bytes_accessed=0, transcendentals=0
        ),
        name="attend",
    )(*scalars, *given)


def first_parts_kernel(k_ref, v_ref, q_ref, out_ref, held_ref, in_sems, out_sems, *, head_count, width):
    kv_width, q_width = k_ref.shape[1] // head_count, q_ref.shape[1] // head_count
    rows = q_ref.shape[0]

    def fetches(h):
        pieces = (
            (k_ref, h * kv_width, 0, kv_width),
            (v_ref, h * kv_width, kv_width, kv_width),
            (q_ref, h * q_width, 2 * kv_width, width),
        )
        return [
            pltpu.make_async_copy(
                ref.at[:, pl.ds(at, size)], held_ref.at[h, :, pl.ds(to, size)], in_sems.at[h, i]
            )
            for i, (ref, at, to, size) in enumerate(pieces)
        ]

    def store(h):
        return pltpu.make_async_copy(held_ref.at[h], out_ref.at[h], out_sems.at[h])

    for h in range(head_count):
        for fetch in fetches(h):
            fetch.start()
    for h in range(head_count):
        for fetch in fetches(h):
            fetch.wait()
        store(h).start()
    for h in range(head_count):
        store(h).wait()


def first_parts(key, value, query, head_count, width):
    shape = (head_count, query.shape[0], 2 * key.shape[1] // head_count + width)
    return pl.pallas_call(
        functools.partial(first_parts_kernel, head_count=head_count, width=width),
        in_specs=[pl.BlockSpec(memory_space=pl.ANY)] * 3,
        out_specs=pl.BlockSpec(memory_space=pl.ANY),
        out_shape=jax.ShapeDtypeStruct(shape, jnp.bfloat16),
        scratch_shapes=[
            pltpu.VMEM(shape, jnp.bfloat16),
            pltpu.SemaphoreType.DMA((head_count, 3)),
            pltpu.SemaphoreType.DMA((head_count,)),
        ],
        compiler_params=pltpu.CompilerParams(vmem_limit_bytes=VMEM_BYTES),
        name="first_parts",
    )(key, value, query)


def later_parts_kernel(place_ref, q_ref, *refs, chips, firsts, widths):
    chunks = len(widths)
    in_sems, out_sems = refs[-2:]
    held_refs, out_refs = refs[-2 - chunks : -2], refs[: -2 - chunks]
    core, chip = place_ref[0], place_ref[1]
    q_width = q_ref.shape[1] // (2 * chips)
    moves = []
    for chunk, (first, width) in enumerate(zip(firsts, widths)):
        outs = out_refs[chunk * (chips + 1) : (chunk + 1) * (chips + 1)]
        for side in range(2):
            for step in range(chips):
                member = lax.rem(chip + step, chips) * 2 + lax.rem(core + side, 2)
                column = pl.multiple_of(member * q_width + first, HD)
                held = held_refs[chunk].at[side * chips + step]
                at = (chunk * 2 + side) * chips + step
                out = outs[chips].at[step] if side else outs[step].at[0]
                moves.append((
                    pltpu.make_async_copy(q_ref.at[:, pl.ds(column, width)], held, in_sems.at[at]),
                    pltpu.make_async_copy(held, out, out_sems.at[at]),
                ))
    for fetch, _ in moves:
        fetch.start()
    for fetch, store in moves:
        fetch.wait()
        store.start()
    for _, store in moves:
        store.wait()


def later_parts(query, place, head_count, firsts, widths):
    rows, chips = query.shape[0], head_count // 2
    shapes = []
    for width in widths:
        shapes += [jax.ShapeDtypeStruct((2, rows, width), jnp.bfloat16)] * chips
        shapes.append(jax.ShapeDtypeStruct((chips, rows, width), jnp.bfloat16))
    copies = 2 * chips * len(widths)
    outs = pl.pallas_call(
        functools.partial(later_parts_kernel, chips=chips, firsts=firsts, widths=widths),
        in_specs=[pl.BlockSpec(memory_space=pltpu.SMEM), pl.BlockSpec(memory_space=pl.ANY)],
        out_specs=[pl.BlockSpec(memory_space=pl.ANY)] * len(shapes),
        out_shape=shapes,
        scratch_shapes=[pltpu.VMEM((2 * chips, rows, width), jnp.bfloat16) for width in widths]
        + [pltpu.SemaphoreType.DMA((copies,))] * 2,
        compiler_params=pltpu.CompilerParams(vmem_limit_bytes=VMEM_BYTES),
        cost_estimate=pl.CostEstimate(flops=0, bytes_accessed=4 * query.size, transcendentals=0),
        name="later_parts",
    )(place, query)
    split = [outs[(chips + 1) * i : (chips + 1) * (i + 1)] for i in range(len(widths))]
    return [list(part[:chips]) for part in split], [part[chips] for part in split]


def fill_kernel(got_ref, *refs):
    held_ref, in_sems, out_sems = refs[-3:]
    steps = held_ref.shape[0]
    out_refs = refs[steps : 2 * steps]
    fetches = [pltpu.make_async_copy(got_ref.at[i], held_ref.at[i], in_sems.at[i]) for i in range(steps)]
    stores = [pltpu.make_async_copy(held_ref.at[i], out_refs[i].at[1], out_sems.at[i]) for i in range(steps)]
    for fetch in fetches:
        fetch.start()
    for fetch, store in zip(fetches, stores):
        fetch.wait()
        store.start()
    for store in stores:
        store.wait()


def fill(parts, got):
    return pl.pallas_call(
        fill_kernel,
        in_specs=[pl.BlockSpec(memory_space=pl.ANY)] * (1 + len(parts)),
        out_specs=[pl.BlockSpec(memory_space=pl.ANY)] * len(parts),
        out_shape=[jax.ShapeDtypeStruct(part.shape, part.dtype) for part in parts],
        scratch_shapes=[pltpu.VMEM(got.shape, got.dtype)] + [pltpu.SemaphoreType.DMA((len(parts),))] * 2,
        input_output_aliases={1 + i: i for i in range(len(parts))},
        compiler_params=pltpu.CompilerParams(vmem_limit_bytes=VMEM_BYTES),
        cost_estimate=pl.CostEstimate(flops=0, bytes_accessed=0, transcendentals=0),
        name="fill",
    )(got, *parts)


def place_kernel(source_ref, *refs, count, first, width):
    received_ref, out_ref, held_ref, in_sems, out_sems = refs[0], refs[-4], refs[-3], refs[-2], refs[-1]

    def fetch(i):
        return pltpu.make_async_copy(received_ref.at[source_ref[i]], held_ref.at[i], in_sems.at[i])

    def store(i):
        return pltpu.make_async_copy(
            held_ref.at[i], out_ref.at[pl.ds(i * BLK, BLK), pl.ds(first, width)], out_sems.at[i]
        )

    for i in range(count):
        fetch(i).start()
    for i in range(count):
        fetch(i).wait()
        store(i).start()
    for i in range(count):
        store(i).wait()


def place(received, source, result, first, count, full_width):
    slots, _, width = received.shape
    given = [received] if result is None else [received, result]
    return pl.pallas_call(
        functools.partial(place_kernel, count=count, first=first, width=width),
        in_specs=[pl.BlockSpec(memory_space=pltpu.SMEM)] + [pl.BlockSpec(memory_space=pl.ANY)] * len(given),
        out_specs=pl.BlockSpec(memory_space=pl.ANY),
        out_shape=jax.ShapeDtypeStruct((count * BLK, full_width), jnp.bfloat16),
        scratch_shapes=[
            pltpu.VMEM((count, BLK, width), jnp.bfloat16),
            pltpu.SemaphoreType.DMA((count,)),
            pltpu.SemaphoreType.DMA((count,)),
        ],
        input_output_aliases={} if result is None else {2: 0},
        compiler_params=pltpu.CompilerParams(vmem_limit_bytes=SHARED_VMEM_BYTES),
        cost_estimate=pl.CostEstimate(flops=0, bytes_accessed=4 * count * BLK * width, transcendentals=0),
        name="place",
    )(source, *given)


def shards(query, key, value, doc_ids, plan):
    head_count = lax.axis_size("head")
    shard_count = lax.axis_size("ctx")
    local_rows = query.shape[0]
    rows = head_count * local_rows
    count = rows // BLK
    per_device = local_rows // BLK
    q_width = query.shape[1] // head_count
    shard = lax.axis_index("ctx").astype(jnp.int32)
    member = lax.axis_index("head").astype(jnp.int32)
    core, chip, chips = member % 2, member // 2, head_count // 2

    widths = [heads * HD for heads in CHUNKS]
    firsts = [sum(widths[:i]) for i in range(len(widths))]
    opening = first_parts(key, value, query, head_count, widths[0])
    kept, given = later_parts(query, jnp.stack([core, chip]), head_count, firsts[1:], widths[1:])
    swap = [(h, h ^ 1) for h in range(head_count)]
    later = [fill(parts, lax.ppermute(part, "head", swap)) for parts, part in zip(kept, given)]
    opening = lax.all_to_all(opening, "head", split_axis=0, concat_axis=0, tiled=True)

    index = jnp.arange(count, dtype=jnp.int32)
    own_ids = shard * count + index
    position = jnp.arange(plan.shape[0], dtype=jnp.int32)
    target = jnp.sum(
        jnp.where(plan[None, :] == own_ids[:, None], position[None, :] // count, 0), axis=1, dtype=jnp.int32
    )
    source = lax.dynamic_slice_in_dim(plan, shard * count, count) // count
    step_of, rest = index // (2 * per_device), index % (2 * per_device)
    giver = (chip - step_of + chips) % chips * 2 + (core + rest // per_device) % 2
    arrival = giver * per_device + rest % per_device

    opening, later, target, source, arrival = lax.optimization_barrier(
        (opening, later, target, source, arrival)
    )
    opening = opening.reshape(rows, 2 * HD + widths[0])
    halo = lax.ppermute(
        opening[rows - HALO * BLK :, : 2 * HD], "ctx", [(i, i + 1) for i in range(shard_count - 1)]
    )
    tables = (doc_ids, target, shard.reshape(1))

    result = None
    for turn, heads in enumerate(CHUNKS):
        if turn == 0:
            views = [(-1, None, i * BLK, 2 * HD) for i in range(count)]
            sent = attend(
                opening, None, [], views[MAXDOC:], None, heads, tables, count, shard_count, MAXDOC, count - MAXDOC
            )
            sent = attend(
                opening, halo, [], views[:MAXDOC], None, heads, tables, count, shard_count, 0, MAXDOC, sent
            )
        else:
            parts = later[turn - 1]
            if turn > 1:
                parts, _ = lax.optimization_barrier((parts, sent))
            sources = []
            for step, part in enumerate(parts):
                onward = [(h, (h + 2 * step) % head_count) for h in range(head_count)]
                sources.append(lax.ppermute(part, "head", onward) if step else part)
            views = [
                (i // (2 * per_device), i // per_device % 2, i % per_device * BLK, 0) for i in range(count)
            ]
            sent = attend(opening, halo, sources, views, arrival, heads, tables, count, shard_count)
        received = lax.all_to_all(sent, "ctx", split_axis=0, concat_axis=0, tiled=True)
        result = place(received, source, result, firsts[turn], count, q_width)
    return result


def solution(mesh):
    return jax.shard_map(
        shards,
        mesh=mesh,
        in_specs=(
            P(("ctx", "head"), None),
            P(("ctx", "head"), None),
            P(("ctx", "head"), None),
            P(),
            P(),
        ),
        out_specs=P("ctx", "head"),
        check_vma=False,
    )
```

```python
import functools
import math

import jax
import jax.numpy as jnp
from jax import lax
from jax.experimental import pallas as pl
from jax.experimental.pallas import tpu as pltpu
from jax.sharding import PartitionSpec as P

HD = 128
BLK = 128
MAXDOC = 8
VMEM_BYTES = 60 * 1024 * 1024
SHARED_VMEM_BYTES = 32 * 1024 * 1024
HALO = MAXDOC - 1
CHUNKS = (2, 6)
EXP2_SCALE = math.log2(math.e) / math.sqrt(HD)


def attend_kernel(doc_ref, slot_ref, shard_ref, *refs, heads, count, base, steps, ahead, paired, ordered, q_views):
    order_ref, refs = (refs[0], refs[1:]) if ordered else (None, refs)
    given, (out_ref, win_ref, held_ref, mixed_ref, kv_sems, q_sems, out_sems) = refs[:-7], refs[-7:]
    width = heads * HD
    own_ref = given[0]

    def copy_own():
        rows = (base + steps) * BLK
        return pltpu.make_async_copy(
            own_ref.at[pl.ds(0, rows), pl.ds(0, 2 * HD)], win_ref.at[pl.ds(ahead * BLK, rows)], kv_sems.at[0]
        )

    def copy_halo():
        return pltpu.make_async_copy(given[1], win_ref.at[pl.ds(0, ahead * BLK)], kv_sems.at[1])

    def copy_out(step):
        return pltpu.make_async_copy(
            mixed_ref.at[step], out_ref.at[slot_ref[base + step]], out_sems.at[step]
        )

    copy_own().start()
    if ahead:
        copy_halo().start()
    for view in range(steps):
        which, lead, row, column = q_views[view]
        source = given[which] if lead is None else given[which].at[lead]
        step = order_ref[view] if ordered else view
        pltpu.make_async_copy(
            source.at[pl.ds(row, BLK), pl.ds(column, width)], held_ref.at[step], q_sems.at[step]
        ).start()

    row = lax.broadcasted_iota(jnp.int32, (heads * BLK, BLK), 0) % BLK
    column = lax.broadcasted_iota(jnp.int32, (heads * BLK, BLK), 1)
    causal = column <= row
    copy_own().wait()
    if ahead:
        copy_halo().wait()

    lanes = 2 if paired else 1

    def per_turn(turn, _):
        at = lanes * turn
        first = base + at
        block = shard_ref[0] * count + first
        doc = doc_ref[block]
        tiles = jnp.int32(1)
        for back in range(1, MAXDOC):
            before = jnp.maximum(block - back, 0)
            tiles += jnp.where((block >= back) & (doc_ref[before] == doc), 1, 0)
        for lane in range(lanes):
            held = held_ref.at[at + lane]
            pltpu.make_async_copy(held, held, q_sems.at[at + lane]).wait()

        def with_tiles(tiles_of):
            windows = []
            for lane, n in enumerate(tiles_of):
                start = pl.multiple_of((first + lane + ahead + 1 - n) * BLK, BLK)
                windows.append(pl.ds(start, n * BLK))
            scores = []
            for lane, n in enumerate(tiles_of):
                queries = jnp.concatenate(
                    [held_ref[at + lane, :, head * HD : (head + 1) * HD] for head in range(heads)], axis=0
                )
                scores.append(lax.dot_general(
                    queries, win_ref[windows[lane], :HD], (((1,), (1,)), ((), ())),
                    preferred_element_type=jnp.float32,
                ))
            for lane, n in enumerate(tiles_of):
                last = jnp.where(causal, scores[lane][:, (n - 1) * BLK :], -jnp.inf)
                scores[lane] = (
                    last if n == 1 else jnp.concatenate([scores[lane][:, : (n - 1) * BLK], last], axis=1)
                )
            tops = [jnp.max(s, axis=1, keepdims=True) for s in scores]
            expos = [jnp.exp2((s - top) * EXP2_SCALE) for s, top in zip(scores, tops)]
            totals = [jnp.sum(e, axis=1, keepdims=True) for e in expos]
            sums = [
                jnp.dot(e.astype(jnp.bfloat16), win_ref[window, HD:], preferred_element_type=jnp.float32)
                for e, window in zip(expos, windows)
            ]
            for lane in range(len(tiles_of)):
                mixed = (sums[lane] / totals[lane]).astype(jnp.bfloat16)
                for head in range(heads):
                    mixed_ref[at + lane, :, head * HD : (head + 1) * HD] = mixed[head * BLK : (head + 1) * BLK]

        if paired:
            same = doc_ref[block + 1] == doc
            for n in range(1, MAXDOC + 1):
                if n < MAXDOC:
                    pl.when((tiles == n) & same)(functools.partial(with_tiles, (n, n + 1)))
                pl.when((tiles == n) & jnp.logical_not(same))(functools.partial(with_tiles, (n, 1)))
        else:
            for n in range(1, MAXDOC + 1):
                pl.when(tiles == n)(functools.partial(with_tiles, (n,)))
        for lane in range(lanes):
            copy_out(at + lane).start()
        return 0

    lax.fori_loop(0, steps // lanes, per_turn, 0)
    for step in range(steps):
        copy_out(step).wait()


def attend(own, halo, sources, q_views, order, heads, tables, count, slots, base=0, steps=None, result=None):
    doc_ids, slot, shard = tables
    steps = count if steps is None else steps
    width = heads * HD
    ahead = 0 if halo is None else HALO
    alone = steps < count
    given = [own] + ([] if halo is None else [halo])
    views = [(len(given) + which if which >= 0 else 0, lead, row, column) for which, lead, row, column in q_views]
    given = given + list(sources) + ([] if result is None else [result])
    scalars = [doc_ids, slot, shard] + ([] if order is None else [order])
    smem, anywhere = pl.BlockSpec(memory_space=pltpu.SMEM), pl.BlockSpec(memory_space=pl.ANY)
    return pl.pallas_call(
        functools.partial(
            attend_kernel, heads=heads, count=count, base=base, steps=steps, ahead=ahead, paired=alone,
            ordered=order is not None, q_views=views
        ),
        in_specs=[smem] * len(scalars) + [anywhere] * len(given),
        out_specs=pl.BlockSpec(memory_space=pl.ANY),
        out_shape=jax.ShapeDtypeStruct((slots, BLK, width), jnp.bfloat16),
        scratch_shapes=[
            pltpu.VMEM(((base + steps + ahead) * BLK, 2 * HD), jnp.bfloat16),
            pltpu.VMEM((steps, BLK, width), jnp.bfloat16),
            pltpu.VMEM((steps, BLK, width), jnp.bfloat16),
            pltpu.SemaphoreType.DMA((2,)),
            pltpu.SemaphoreType.DMA((steps,)),
            pltpu.SemaphoreType.DMA((steps,)),
        ],
        input_output_aliases={} if result is None else {len(scalars) + len(given) - 1: 0},
        compiler_params=pltpu.CompilerParams(vmem_limit_bytes=VMEM_BYTES if alone else SHARED_VMEM_BYTES),
        cost_estimate=pl.CostEstimate(
            flops=10**12 if ahead else 0, bytes_accessed=0, transcendentals=0
        ),
        name="attend",
    )(*scalars, *given)


def first_parts_kernel(k_ref, v_ref, q_ref, out_ref, held_ref, in_sems, out_sems, *, head_count, width):
    kv_width, q_width = k_ref.shape[1] // head_count, q_ref.shape[1] // head_count
    rows = q_ref.shape[0]

    def fetches(h):
        pieces = (
            (k_ref, h * kv_width, 0, kv_width),
            (v_ref, h * kv_width, kv_width, kv_width),
            (q_ref, h * q_width, 2 * kv_width, width),
        )
        return [
            pltpu.make_async_copy(
                ref.at[:, pl.ds(at, size)], held_ref.at[h, :, pl.ds(to, size)], in_sems.at[h, i]
            )
            for i, (ref, at, to, size) in enumerate(pieces)
        ]

    def store(h):
        return pltpu.make_async_copy(held_ref.at[h], out_ref.at[h], out_sems.at[h])

    for h in range(head_count):
        for fetch in fetches(h):
            fetch.start()
    for h in range(head_count):
        for fetch in fetches(h):
            fetch.wait()
        store(h).start()
    for h in range(head_count):
        store(h).wait()


def first_parts(key, value, query, head_count, width):
    shape = (head_count, query.shape[0], 2 * key.shape[1] // head_count + width)
    return pl.pallas_call(
        functools.partial(first_parts_kernel, head_count=head_count, width=width),
        in_specs=[pl.BlockSpec(memory_space=pl.ANY)] * 3,
        out_specs=pl.BlockSpec(memory_space=pl.ANY),
        out_shape=jax.ShapeDtypeStruct(shape, jnp.bfloat16),
        scratch_shapes=[
            pltpu.VMEM(shape, jnp.bfloat16),
            pltpu.SemaphoreType.DMA((head_count, 3)),
            pltpu.SemaphoreType.DMA((head_count,)),
        ],
        compiler_params=pltpu.CompilerParams(vmem_limit_bytes=VMEM_BYTES),
        name="first_parts",
    )(key, value, query)


def later_parts_kernel(place_ref, q_ref, *refs, chips, firsts, widths):
    chunks = len(widths)
    in_sems, out_sems = refs[-2:]
    held_refs, out_refs = refs[-2 - chunks : -2], refs[: -2 - chunks]
    core, chip = place_ref[0], place_ref[1]
    q_width = q_ref.shape[1] // (2 * chips)
    moves = []
    for chunk, (first, width) in enumerate(zip(firsts, widths)):
        outs = out_refs[chunk * (chips + 1) : (chunk + 1) * (chips + 1)]
        for side in range(2):
            for step in range(chips):
                member = lax.rem(chip + step, chips) * 2 + lax.rem(core + side, 2)
                column = pl.multiple_of(member * q_width + first, HD)
                held = held_refs[chunk].at[side * chips + step]
                at = (chunk * 2 + side) * chips + step
                out = outs[chips].at[step] if side else outs[step].at[0]
                moves.append((
                    pltpu.make_async_copy(q_ref.at[:, pl.ds(column, width)], held, in_sems.at[at]),
                    pltpu.make_async_copy(held, out, out_sems.at[at]),
                ))
    for fetch, _ in moves:
        fetch.start()
    for fetch, store in moves:
        fetch.wait()
        store.start()
    for _, store in moves:
        store.wait()


def later_parts(query, place, head_count, firsts, widths):
    rows, chips = query.shape[0], head_count // 2
    shapes = []
    for width in widths:
        shapes += [jax.ShapeDtypeStruct((2, rows, width), jnp.bfloat16)] * chips
        shapes.append(jax.ShapeDtypeStruct((chips, rows, width), jnp.bfloat16))
    copies = 2 * chips * len(widths)
    outs = pl.pallas_call(
        functools.partial(later_parts_kernel, chips=chips, firsts=firsts, widths=widths),
        in_specs=[pl.BlockSpec(memory_space=pltpu.SMEM), pl.BlockSpec(memory_space=pl.ANY)],
        out_specs=[pl.BlockSpec(memory_space=pl.ANY)] * len(shapes),
        out_shape=shapes,
        scratch_shapes=[pltpu.VMEM((2 * chips, rows, width), jnp.bfloat16) for width in widths]
        + [pltpu.SemaphoreType.DMA((copies,))] * 2,
        compiler_params=pltpu.CompilerParams(vmem_limit_bytes=VMEM_BYTES),
        cost_estimate=pl.CostEstimate(flops=0, bytes_accessed=4 * query.size, transcendentals=0),
        name="later_parts",
    )(place, query)
    split = [outs[(chips + 1) * i : (chips + 1) * (i + 1)] for i in range(len(widths))]
    return [list(part[:chips]) for part in split], [part[chips] for part in split]


def fill_kernel(got_ref, *refs):
    held_ref, in_sems, out_sems = refs[-3:]
    steps = held_ref.shape[0]
    out_refs = refs[steps : 2 * steps]
    fetches = [pltpu.make_async_copy(got_ref.at[i], held_ref.at[i], in_sems.at[i]) for i in range(steps)]
    stores = [pltpu.make_async_copy(held_ref.at[i], out_refs[i].at[1], out_sems.at[i]) for i in range(steps)]
    for fetch in fetches:
        fetch.start()
    for fetch, store in zip(fetches, stores):
        fetch.wait()
        store.start()
    for store in stores:
        store.wait()


def fill(parts, got):
    return pl.pallas_call(
        fill_kernel,
        in_specs=[pl.BlockSpec(memory_space=pl.ANY)] * (1 + len(parts)),
        out_specs=[pl.BlockSpec(memory_space=pl.ANY)] * len(parts),
        out_shape=[jax.ShapeDtypeStruct(part.shape, part.dtype) for part in parts],
        scratch_shapes=[pltpu.VMEM(got.shape, got.dtype)] + [pltpu.SemaphoreType.DMA((len(parts),))] * 2,
        input_output_aliases={1 + i: i for i in range(len(parts))},
        compiler_params=pltpu.CompilerParams(vmem_limit_bytes=VMEM_BYTES),
        cost_estimate=pl.CostEstimate(flops=0, bytes_accessed=0, transcendentals=0),
        name="fill",
    )(got, *parts)


def place_kernel(source_ref, *refs, count, first, width):
    received_ref, out_ref, held_ref, in_sems, out_sems = refs[0], refs[-4], refs[-3], refs[-2], refs[-1]

    half = BLK // 2

    def fetch(i):
        rows = pl.ds(i % 2 * half, half)
        return pltpu.make_async_copy(
            received_ref.at[source_ref[i // 2], rows], held_ref.at[i // 2, rows], in_sems.at[i]
        )

    def store(i):
        rows = pl.ds(i % 2 * half, half)
        return pltpu.make_async_copy(
            held_ref.at[i // 2, rows], out_ref.at[pl.ds(i * half, half), pl.ds(first, width)], out_sems.at[i]
        )

    for i in range(2 * count):
        fetch(i).start()
    for i in range(2 * count):
        fetch(i).wait()
        store(i).start()
    for i in range(2 * count):
        store(i).wait()


def place(received, source, result, first, count, full_width):
    slots, _, width = received.shape
    given = [received] if result is None else [received, result]
    return pl.pallas_call(
        functools.partial(place_kernel, count=count, first=first, width=width),
        in_specs=[pl.BlockSpec(memory_space=pltpu.SMEM)] + [pl.BlockSpec(memory_space=pl.ANY)] * len(given),
        out_specs=pl.BlockSpec(memory_space=pl.ANY),
        out_shape=jax.ShapeDtypeStruct((count * BLK, full_width), jnp.bfloat16),
        scratch_shapes=[
            pltpu.VMEM((count, BLK, width), jnp.bfloat16),
            pltpu.SemaphoreType.DMA((2 * count,)),
            pltpu.SemaphoreType.DMA((2 * count,)),
        ],
        input_output_aliases={} if result is None else {2: 0},
        compiler_params=pltpu.CompilerParams(vmem_limit_bytes=SHARED_VMEM_BYTES),
        cost_estimate=pl.CostEstimate(flops=0, bytes_accessed=4 * count * BLK * width, transcendentals=0),
        name="place",
    )(source, *given)


def shards(query, key, value, doc_ids, plan):
    head_count = lax.axis_size("head")
    shard_count = lax.axis_size("ctx")
    local_rows = query.shape[0]
    rows = head_count * local_rows
    count = rows // BLK
    per_device = local_rows // BLK
    q_width = query.shape[1] // head_count
    shard = lax.axis_index("ctx").astype(jnp.int32)
    member = lax.axis_index("head").astype(jnp.int32)
    core, chip, chips = member % 2, member // 2, head_count // 2

    widths = [heads * HD for heads in CHUNKS]
    firsts = [sum(widths[:i]) for i in range(len(widths))]
    opening = first_parts(key, value, query, head_count, widths[0])
    kept, given = later_parts(query, jnp.stack([core, chip]), head_count, firsts[1:], widths[1:])
    swap = [(h, h ^ 1) for h in range(head_count)]
    later = [fill(parts, lax.ppermute(part, "head", swap)) for parts, part in zip(kept, given)]
    opening = lax.all_to_all(opening, "head", split_axis=0, concat_axis=0, tiled=True)

    index = jnp.arange(count, dtype=jnp.int32)
    own_ids = shard * count + index
    position = jnp.arange(plan.shape[0], dtype=jnp.int32)
    target = jnp.sum(
        jnp.where(plan[None, :] == own_ids[:, None], position[None, :] // count, 0), axis=1, dtype=jnp.int32
    )
    source = lax.dynamic_slice_in_dim(plan, shard * count, count) // count
    step_of, rest = index // (2 * per_device), index % (2 * per_device)
    giver = (chip - step_of + chips) % chips * 2 + (core + rest // per_device) % 2
    arrival = giver * per_device + rest % per_device

    opening, later, target, source, arrival = lax.optimization_barrier(
        (opening, later, target, source, arrival)
    )
    opening = opening.reshape(rows, 2 * HD + widths[0])
    halo = lax.ppermute(
        opening[rows - HALO * BLK :, : 2 * HD], "ctx", [(i, i + 1) for i in range(shard_count - 1)]
    )
    tables = (doc_ids, target, shard.reshape(1))

    result = None
    for turn, heads in enumerate(CHUNKS):
        if turn == 0:
            views = [(-1, None, i * BLK, 2 * HD) for i in range(count)]
            sent = attend(
                opening, None, [], views[MAXDOC:], None, heads, tables, count, shard_count, MAXDOC, count - MAXDOC
            )
            sent = attend(
                opening, halo, [], views[:MAXDOC], None, heads, tables, count, shard_count, 0, MAXDOC, sent
            )
        else:
            sources = []
            for step, part in enumerate(later[turn - 1]):
                onward = [(h, (h + 2 * step) % head_count) for h in range(head_count)]
                sources.append(lax.ppermute(part, "head", onward) if step else part)
            views = [
                (i // (2 * per_device), i // per_device % 2, i % per_device * BLK, 0) for i in range(count)
            ]
            sent = attend(opening, halo, sources, views, arrival, heads, tables, count, shard_count)
        received = lax.all_to_all(sent, "ctx", split_axis=0, concat_axis=0, tiled=True)
        result = place(received, source, result, firsts[turn], count, q_width)
    return result


def solution(mesh):
    return jax.shard_map(
        shards,
        mesh=mesh,
        in_specs=(
            P(("ctx", "head"), None),
            P(("ctx", "head"), None),
            P(("ctx", "head"), None),
            P(),
            P(),
        ),
        out_specs=P("ctx", "head"),
        check_vma=False,
    )
```
